32 devices in a mesh: parts: 2 (over x), col: 16 (over z, y, core).
Axes of the slice: x: 2, y: 2, z: 4, core: 2. Of those that a mesh axis runs over, the one named last changes fastest.
Arguments:
- outages: int32 [2048], P(('parts', 'col')), parts along dimension 0, may hold values from 0 to 20479
- branch_from: int32 [20480], replicated, may hold values from 0 to 8191
- branch_to: int32 [20480], replicated, may hold values from 0 to 8191, as said below
- bus_slot: int32 [8192], replicated, may hold values from 0 to 8191, each once
- susceptance: float32 [20480], replicated, may hold values from 0.03 to 0.09
- charging: float32 [20480], replicated, may hold values from 0.04 to 0.12
- rating: float32 [20480], replicated, may hold values from 0.018 to 0.063
- base_angles: float32 [16384], P('parts'), parts along dimension 0, may hold values from -1.2 to 1.2
- zinv: float32 [8192, 8192], P(None, 'col'), may hold values from -0.6 to 2, as said below
Outputs:
- injections: float32 [2, 2048], P(None, ('parts', 'col')), parts along dimension 1
- deviation: float32 [2048, 8192], P('parts', 'col'), parts along dimension 0
- worst: float32 [2048], P(('parts', 'col')), parts along dimension 0
The draws below stay inside these ranges and needn't reach their ends.
There are 2 independent parts, one for each index of `parts`. The reference program is written for one: setup_inputs(seed, part) draws one part's arguments, and reference() takes and returns one part's arrays. A program takes and returns all parts, laid end to end along the dimension named above; an argument that names none is the same for every part. Nothing has to cross between parts.
Inputs may be any that keep to these rules, and one draw needn't show every extreme that they name: branch_to differs from branch_from on every branch. zinv is symmetric; its diagonal lies in [1, 2] and every other entry in [-0.6, 0.6].
All inputs are finite; a program needn't handle non-finite values.
Results may differ from the reference program's by a relative error of at most 0.0003.
Values sent between devices are 32-bit elements; how exact they have to be, the bound alone decides.
No kernel may reach another device: no remote copies, remote signals or barrier semaphores. Data moves between devices by JAX's collectives and lax.ppermute only.
A program may use at most 128 MiB of HBM per device.

```python
import math
import jax
import jax.numpy as jnp
from jax import lax

NB = 8192
NBR = 20480
STEPS = 3
NOUT = 1024


def branch_pair(key):
    inner = jax.random.fold_in(key, 7)
    first_key, second_key = jax.random.split(inner)
    head = jax.random.randint(first_key, (NBR,), 0, NB, dtype=jnp.int32)
    offset = jax.random.randint(second_key, (NBR,), 1, NB, dtype=jnp.int32)
    return (head, (head + offset) % NB)


def draw_branch_from(key, part):
    return branch_pair(key)[0]


def draw_branch_to(key, part):
    return branch_pair(key)[1]


def line_pair(key, low_ratio, high_ratio):
    inner = jax.random.fold_in(key, 13)
    first_key, second_key = jax.random.split(inner)
    suscept = jnp.exp(jax.random.uniform(first_key, (NBR,), jnp.float32, math.log(0.03), math.log(0.09)))
    suscept = jnp.clip(suscept, 0.03, 0.09)
    ratio = jax.random.uniform(second_key, (NBR,), jnp.float32, low_ratio, high_ratio)
    limit = jnp.clip(suscept * ratio, 0.018, 0.063)
    return (suscept.astype(jnp.float32), limit.astype(jnp.float32))


def draw_susceptance(key, part):
    return line_pair(key, 0.6, 0.7)[0]


def draw_rating(key, part):
    return line_pair(key, 0.6, 0.7)[1]


def draw_base_angles(key, part):
    key = jax.random.fold_in(key, 5)
    sign_key, level_key, noise_key = jax.random.split(key, 3)
    sign_val = 2.0 * jax.random.randint(sign_key, (), 0, 2, dtype=jnp.int32).astype(jnp.float32) - 1.0
    offset = jax.random.uniform(level_key, (), jnp.float32, 0.8, 1.1)
    noise = jax.random.uniform(noise_key, (NB,), jnp.float32, -0.03, 0.03)
    return jnp.clip(sign_val * offset + noise, -1.2, 1.2).astype(jnp.float32)


def draw_zinv(key, part):
    first_key, second_key = jax.random.split(jax.random.fold_in(key, 11))
    raw = 0.3 * jax.random.truncated_normal(first_key, -2.0, 2.0, (NB, NB), jnp.float32)
    diagonal = jax.random.uniform(second_key, (NB,), jnp.float32, 1.0, 2.0)
    symmetric = 0.5 * (raw + raw.T)
    index = jnp.arange(NB, dtype=jnp.int32)
    on_diag = index[:, None] == index[None, :]
    return jnp.where(on_diag, diagonal[:, None] * jnp.ones_like(symmetric), symmetric).astype(jnp.float32)


def place_ends(result, stream_key, smallest, high):
    place = [jax.random.randint(jax.random.fold_in(stream_key, axis), (), 0, length) for axis, length in enumerate(result.shape)]
    main_axis = result.shape.index(max(result.shape))
    neighbour = place[:main_axis] + [(place[main_axis] + 1) % result.shape[main_axis]] + place[main_axis + 1:]
    return result.at[tuple(place)].set(smallest).at[tuple(neighbour)].set(high)


def setup_inputs(seed: int = 0, part: int = 0) -> dict:
    arg_keys = jax.random.split(jax.random.key(seed), 10)
    part_splits = jax.random.split(jax.random.fold_in(arg_keys[9], part), 10)
    return {
        "outages": place_ends(jax.random.randint(part_splits[0], (NOUT,), 0, NBR), jax.random.fold_in(part_splits[0], 1), 0, NBR - 1).astype(jnp.int32),
        "branch_from": draw_branch_from(jax.random.fold_in(arg_keys[9], 71), part),
        "branch_to": draw_branch_to(jax.random.fold_in(arg_keys[9], 71), part),
        "bus_slot": jax.random.permutation(arg_keys[3], NB).astype(jnp.int32),
        "susceptance": draw_susceptance(jax.random.fold_in(arg_keys[9], 71), part),
        "charging": jnp.clip(jnp.exp(jax.random.uniform(arg_keys[5], (NBR,), jnp.float32, math.log(0.04), math.log(0.12))), 0.04, 0.12),
        "rating": draw_rating(jax.random.fold_in(arg_keys[9], 71), part),
        "base_angles": draw_base_angles(jax.random.fold_in(jax.random.fold_in(arg_keys[9], part), 71), part),
        "zinv": draw_zinv(jax.random.fold_in(arg_keys[9], 71), part),
    }


def newton(a_head, a_tail, self_head, cross_head, cross_tail, self_tail, bsus, hchg):
    inj_head = jnp.zeros_like(a_head)
    inj_tail = jnp.zeros_like(a_head)
    for step in range(1, STEPS + 1):
        level = step / STEPS
        end_head = a_head + self_head * inj_head + cross_head * inj_tail
        end_tail = a_tail + cross_tail * inj_head + self_tail * inj_tail
        spread = end_head - end_tail
        sine_val = jnp.sin(spread)
        cosine_val = jnp.cos(spread)
        resid_head = inj_head - level * (bsus * sine_val + hchg * end_head)
        resid_tail = inj_tail - level * (-bsus * sine_val + hchg * end_tail)
        diag_term = bsus * cosine_val + hchg
        cross_term = -bsus * cosine_val
        jac_one = 1.0 - level * (diag_term * self_head + cross_term * cross_tail)
        jac_two = -level * (diag_term * cross_head + cross_term * self_tail)
        jac_three = -level * (cross_term * self_head + diag_term * cross_tail)
        jac_four = 1.0 - level * (cross_term * cross_head + diag_term * self_tail)
        determinant = jac_one * jac_four - jac_two * jac_three
        inj_head = inj_head - (jac_four * resid_head - jac_two * resid_tail) / determinant
        inj_tail = inj_tail - (jac_one * resid_tail - jac_three * resid_head) / determinant
    return inj_head, inj_tail


def worst_loading(angles, ids, from_slot, to_slot, susceptance, rating):
    rows_total = angles.shape[0]
    block_rows = math.gcd(rows_total, 32)
    branch_ids = jnp.arange(susceptance.shape[0], dtype=jnp.int32)

    def one_block(packed):
        block, block_ids = packed
        spread = jnp.take(block, from_slot, axis=1) - jnp.take(block, to_slot, axis=1)
        load = jnp.abs(susceptance[None, :] * jnp.sin(spread)) / rating[None, :]
        load = jnp.where(branch_ids[None, :] == block_ids[:, None], jnp.zeros_like(load), load)
        return jnp.max(load, axis=1)

    shaped = angles.reshape(rows_total // block_rows, block_rows, angles.shape[1])
    shaped_ids = ids.reshape(rows_total // block_rows, block_rows)
    return lax.map(one_block, (shaped, shaped_ids)).reshape(rows_total)


def reference(outages, branch_from, branch_to, bus_slot, susceptance, charging, rating, base_angles, zinv):
    from_slot = bus_slot[branch_from]
    to_slot = bus_slot[branch_to]
    head = from_slot[outages]
    tail = to_slot[outages]
    row_head = zinv[head]
    row_tail = zinv[tail]
    self_head = jnp.take_along_axis(row_head, head[:, None], axis=1)[:, 0]
    cross_head = jnp.take_along_axis(row_head, tail[:, None], axis=1)[:, 0]
    cross_tail = jnp.take_along_axis(row_tail, head[:, None], axis=1)[:, 0]
    self_tail = jnp.take_along_axis(row_tail, tail[:, None], axis=1)[:, 0]
    inj_head, inj_tail = newton(base_angles[head], base_angles[tail], self_head, cross_head, cross_tail, self_tail, susceptance[outages], charging[outages])
    deviation = inj_head[:, None] * row_head + inj_tail[:, None] * row_tail
    worst = worst_loading(base_angles[None, :] + deviation, outages, from_slot, to_slot, susceptance, rating)
    return jnp.stack([inj_head, inj_tail]), deviation, worst
```

```python
import functools
import math

import jax
import jax.numpy as jnp
from jax import lax
from jax.experimental import pallas as pl
from jax.experimental.pallas import tpu as pltpu
from jax.sharding import PartitionSpec as P

STEPS = 3
LANES = 128
FIXED = float(2**30)
SINE = (3.1415926444, -5.1677100819, 2.5500775297, -0.5982913039, 0.0776576582)
VMEM = pl.BlockSpec(memory_space=pltpu.VMEM)
SMEM = pl.BlockSpec(memory_space=pltpu.SMEM)
ANY = pl.BlockSpec(memory_space=pl.ANY)


def params(mib):
    return pltpu.CompilerParams(vmem_limit_bytes=mib * 2**20)


def split(table, parts):
    out = []
    for _ in range(parts):
        piece = table.astype(jnp.bfloat16)
        out.append(piece)
        table = table - piece.astype(jnp.float32)
    return out


def lookup(pieces, index):
    rows = pieces[0].shape[0]
    n = index.shape[1]
    hot = lax.broadcasted_iota(jnp.int32, (rows, n), 0) == (index >> 7)
    hot = jnp.where(hot, 1.0, 0.0).astype(jnp.bfloat16)
    dims = (((0,), (0,)), ((), ()))
    total = sum(lax.dot_general(p, hot, dims, preferred_element_type=jnp.float32) for p in pieces)
    lane = lax.broadcasted_iota(jnp.int32, (LANES, n), 0) == (index & 127)
    return jnp.sum(jnp.where(lane, total, 0.0), axis=0, keepdims=True)


def newton(a_head, a_tail, self_head, cross, self_tail, bsus, hchg):
    inj_head = jnp.zeros_like(a_head)
    inj_tail = jnp.zeros_like(a_head)
    for step in range(1, STEPS + 1):
        level = step / STEPS
        end_head = a_head + self_head * inj_head + cross * inj_tail
        end_tail = a_tail + cross * inj_head + self_tail * inj_tail
        spread = end_head - end_tail
        sine_val = jnp.sin(spread)
        cosine_val = jnp.cos(spread)
        resid_head = inj_head - level * (bsus * sine_val + hchg * end_head)
        resid_tail = inj_tail - level * (-bsus * sine_val + hchg * end_tail)
        diag_term = bsus * cosine_val + hchg
        cross_term = -bsus * cosine_val
        jac_one = 1.0 - level * (diag_term * self_head + cross_term * cross)
        jac_two = -level * (diag_term * cross + cross_term * self_tail)
        jac_three = -level * (cross_term * self_head + diag_term * cross)
        jac_four = 1.0 - level * (cross_term * cross + diag_term * self_tail)
        determinant = jac_one * jac_four - jac_two * jac_three
        inj_head = inj_head - (jac_four * resid_head - jac_two * resid_tail) / determinant
        inj_tail = inj_tail - (jac_one * resid_tail - jac_three * resid_head) / determinant
    return inj_head, inj_tail


def ends_kernel(cols, me_ref, ids_ref, from_ref, to_ref, slot_ref, sus_ref, chg_ref, base_ref, zinv_ref,
                head_ref, tail_ref, pick_ref, state_ref, cross_ref, tile_s, rows, tiles, sem):
    blocks = ids_ref.shape[0]
    width = cols // LANES
    first = me_ref[0] * cols
    f_parts = split(from_ref[...].astype(jnp.float32), 2)
    t_parts = split(to_ref[...].astype(jnp.float32), 2)
    s_parts = split(slot_ref[...].astype(jnp.float32), 2)
    sus_parts = split(sus_ref[...], 3)
    chg_parts = split(chg_ref[...], 3)
    base_parts = split(base_ref[...], 3)
    for b in range(blocks):
        row = pl.ds(b, 1)
        ids = ids_ref[row, :]
        head = lookup(s_parts, lookup(f_parts, ids).astype(jnp.int32)).astype(jnp.int32)
        tail = lookup(s_parts, lookup(t_parts, ids).astype(jnp.int32)).astype(jnp.int32)
        head_ref[0, row, :] = head
        tail_ref[0, row, :] = tail
        head_ref[1, row, :] = (head >> 3) * (8 * width) + (head & 7)
        tail_ref[1, row, :] = (tail >> 3) * (8 * width) + (tail & 7)
        state_ref[0, row, :] = lookup(base_parts, head)
        state_ref[1, row, :] = lookup(base_parts, tail)
        state_ref[2, row, :] = lookup(sus_parts, ids)
        state_ref[3, row, :] = lookup(chg_parts, ids)
        pick_ref[row, :] = tail - first
        column = jnp.clip((tail - first) >> 7, 0, width - 1)
        tiles[row, :] = (head >> 3) * (8 * width) + (head & 7) + column * 8
    copy = pltpu.make_async_copy(tiles, tile_s, sem)
    copy.start()
    copy.wait()

    def block(b, carry):
        for j in range(LANES):
            rows[pl.ds(j, 1), :] = zinv_ref[pl.ds(tile_s[b, j], 1), :]
        offset = pick_ref[pl.ds(b, 1), :]
        inside = (offset >= 0) & (offset < cols)
        hit = lax.broadcasted_iota(jnp.int32, (LANES, LANES), 0) == jnp.where(inside, offset & 127, -1)
        entry = jnp.sum(jnp.where(hit, rows[...].T, 0.0), axis=0, keepdims=True)
        cross_ref[pl.ds(b, 1), :] = jnp.round(entry * FIXED).astype(jnp.int32)
        return carry

    lax.fori_loop(0, blocks, block, 0)


def spread_kernel(me_ref, head_s, tail_s, head_ref, tail_ref, state_ref, cross_ref, diag_ref, base_ref,
                  zinv_ref, inj_ref, dev_ref, *rest):
    units, (rows_h, rows_t) = rest[:-2], rest[-2:]
    blocks, cols = cross_ref.shape[0], units[0].shape[0]
    tiles = cols // LANES
    me = me_ref[0]
    chip = me >> 1
    d_parts = split(diag_ref[...], 3)
    self_h = [lookup(d_parts, head_ref[0, pl.ds(b, 1), :]) for b in range(blocks)]
    self_t = [lookup(d_parts, tail_ref[0, pl.ds(b, 1), :]) for b in range(blocks)]
    cross = cross_ref[...].astype(jnp.float32) * (1.0 / FIXED)
    inj_h, inj_t = newton(state_ref[0], state_ref[1], jnp.concatenate(self_h, 0), cross,
                          jnp.concatenate(self_t, 0), state_ref[2], state_ref[3])
    inj_ref[0] = inj_h
    inj_ref[1] = inj_t
    for d, unit in enumerate(units):
        blk = chip ^ d

        def fetch(j, carry):
            for i in range(16):
                o = j * 16 + i
                for t in range(tiles):
                    rows_h[t, pl.ds(o, 1), :] = zinv_ref[pl.ds(head_s[1, blk, o] + 8 * t, 1), :]
                    rows_t[t, pl.ds(o, 1), :] = zinv_ref[pl.ds(tail_s[1, blk, o] + 8 * t, 1), :]
            return carry

        lax.fori_loop(0, LANES // 16, fetch, 0)
        scale_h = jnp.broadcast_to(inj_ref[0, pl.ds(blk, 1), :], (LANES, LANES)).T
        scale_t = jnp.broadcast_to(inj_ref[1, pl.ds(blk, 1), :], (LANES, LANES)).T
        for t in range(tiles):
            at = slice(t * LANES, (t + 1) * LANES)
            dev = scale_h * rows_h[t] + scale_t * rows_t[t]
            dev_ref[pl.ds(pl.multiple_of(blk * LANES, LANES), LANES), at] = dev
            angle = base_ref[pl.ds(me * tiles + t, 1), :] + dev
            unit[at, :] = (angle * (1.0 / math.pi)).T


def prep_kernel(me_ref, from_ref, to_ref, slot_ref, sus_ref, rate_ref, f_ref, t_ref, ratio_ref):
    half = f_ref.shape[0]
    me = me_ref[0]
    start = (me & 1) * half
    flip = me * (slot_ref.shape[0] * LANES // me_ref[1])
    s_parts = split(slot_ref[...].astype(jnp.float32), 2)

    def group(g, carry):
        for i in range(8):
            row = pl.ds(start + g * 8 + i, 1)
            out = pl.ds(g * 8 + i, 1)
            f_ref[out, :] = lookup(s_parts, from_ref[row, :]).astype(jnp.int32) ^ flip
            t_ref[out, :] = lookup(s_parts, to_ref[row, :]).astype(jnp.int32) ^ flip
            ratio_ref[out, :] = sus_ref[row, :] / rate_ref[row, :]
        return carry

    lax.fori_loop(0, half // 8, group, 0)


def worst_kernel(me_ref, f_s, t_s, ratio_ref, ids_ref, *rest):
    pieces, (out_ref, table, diff, best, sem) = rest[:-5], rest[-5:]
    unit = pieces[0].shape[0]
    copies = []
    for i, piece in enumerate(pieces):
        copy = pltpu.make_async_copy(piece, table.at[pl.ds(i * unit, unit)], sem.at[i])
        copy.start()
        copies.append(copy)
    for copy in copies:
        copy.wait()
    half = f_s.shape[0]
    me = me_ref[0]
    ids = ids_ref[pl.ds(me >> 1, 1), :]
    start = (me & 1) * half
    best[...] = jnp.zeros_like(best)

    def block(b, carry):
        for j in range(LANES):
            diff[pl.ds(j, 1), :] = table[pl.ds(f_s[b, j], 1), :] - table[pl.ds(t_s[b, j], 1), :]
        turn = diff[...]
        turn = turn - jnp.round(turn)
        square = turn * turn
        poly = SINE[4]
        for c in SINE[3::-1]:
            poly = poly * square + c
        ratio = jnp.broadcast_to(ratio_ref[pl.ds(b, 1), :], (LANES, LANES)).T
        load = jnp.abs(turn * poly) * ratio
        branch = lax.broadcasted_iota(jnp.int32, (LANES, LANES), 0) + (start + b) * LANES
        load = jnp.where(branch == ids, 0.0, load)
        best[...] = jnp.maximum(best[...], jnp.max(load.reshape(LANES // 8, 8, LANES), axis=0))
        return carry

    lax.fori_loop(0, half, block, 0)
    out_ref[...] = jnp.max(best[...], axis=0, keepdims=True)


def per_device(
    outages, branch_from, branch_to, bus_slot, susceptance, charging, rating, base_angles, zinv
):
    n_col = lax.axis_size("col")
    buses, cols = zinv.shape
    own = outages.shape[0]
    total = own * n_col
    blocks = total // LANES
    chips = n_col // 2
    assert own * 2 == LANES and chips & (chips - 1) == 0
    me = lax.axis_index("col")
    where = jnp.stack([me, jnp.int32(n_col)])
    tab = lambda a: a.reshape(-1, LANES)
    from2, to2, slot2, sus2, chg2, rate2, base2 = map(
        tab, (branch_from, branch_to, bus_slot, susceptance, charging, rating, base_angles)
    )
    i32 = lambda *s: jax.ShapeDtypeStruct(s, jnp.int32)
    f32 = lambda *s: jax.ShapeDtypeStruct(s, jnp.float32)

    flat = zinv.reshape(buses // 8, 8, cols // LANES, LANES).transpose(0, 2, 1, 3).reshape(-1, LANES)
    square = lax.dynamic_slice(zinv, (me * cols, 0), (cols, cols))
    diag = jnp.sum(jnp.where(jnp.eye(cols, dtype=bool), square, 0.0), axis=0)
    diag = tab(lax.all_gather(diag, "col", tiled=True))
    ids = lax.dynamic_update_slice(jnp.zeros((total,), jnp.int32), outages, (me * own,))
    ids = lax.psum(tab(ids), "col")

    head, tail, _, state, cross = pl.pallas_call(
        functools.partial(ends_kernel, cols),
        name="ends",
        out_shape=[i32(2, blocks, LANES), i32(2, blocks, LANES), i32(blocks, LANES),
                   f32(4, blocks, LANES), i32(blocks, LANES)],
        in_specs=[SMEM] + [VMEM] * 8,
        out_specs=[VMEM] * 5,
        scratch_shapes=[pltpu.SMEM((blocks, LANES), jnp.int32), pltpu.VMEM((LANES, LANES), jnp.float32),
                        pltpu.VMEM((blocks, LANES), jnp.int32), pltpu.SemaphoreType.DMA],
        compiler_params=params(24),
    )(where, ids, from2, to2, slot2, sus2, chg2, base2, flat)
    cross = lax.psum(cross, "col")

    injections, deviation, *units = pl.pallas_call(
        spread_kernel,
        name="spread",
        out_shape=[f32(2, blocks, LANES), f32(total, cols)] + [f32(cols, LANES)] * chips,
        in_specs=[SMEM] * 3 + [VMEM] * 7,
        out_specs=[VMEM] * (2 + chips),
        scratch_shapes=[pltpu.VMEM((cols // LANES, LANES, LANES), jnp.float32)] * 2,
        compiler_params=params(32),
    )(where, head, tail, head, tail, state, cross, diag, base2, flat)

    half = from2.shape[0] // 2
    f_rel, t_rel, ratio = pl.pallas_call(
        prep_kernel,
        name="prep",
        out_shape=[i32(half, LANES), i32(half, LANES), f32(half, LANES)],
        in_specs=[SMEM] + [VMEM] * 5,
        out_specs=[VMEM] * 3,
        cost_estimate=pl.CostEstimate(flops=10**9, bytes_accessed=10**6, transcendentals=0),
    )(where, from2, to2, slot2, sus2, rate2)

    far = sorted(range(1, chips), reverse=True)
    got = {0: units[0]}
    for d in far:
        got[d] = lax.ppermute(units[d], "col", [(i, i ^ (2 * d)) for i in range(n_col)])
    pieces = []
    for d in range(chips):
        pieces.append(got[d])
        pieces.append(lax.ppermute(got[d], "col", [(i, i ^ 1) for i in range(n_col)]))

    worst = pl.pallas_call(
        worst_kernel,
        name="worst",
        out_shape=f32(1, LANES),
        in_specs=[SMEM] * 3 + [VMEM] * 2 + [ANY] * n_col,
        out_specs=VMEM,
        scratch_shapes=[pltpu.VMEM((buses, LANES), jnp.float32), pltpu.VMEM((LANES, LANES), jnp.float32),
                        pltpu.VMEM((8, LANES), jnp.float32), pltpu.SemaphoreType.DMA((n_col,))],
        compiler_params=params(16),
    )(where, f_rel, t_rel, ratio, ids, *pieces)
    other = lax.ppermute(worst, "col", [(i, i ^ 1) for i in range(n_col)])
    worst = lax.dynamic_slice(jnp.maximum(worst, other)[0], ((me & 1) * own,), (own,))
    inj = lax.dynamic_slice(injections.reshape(2, total), (0, me * own), (2, own))
    return inj, deviation, worst


def solution(mesh):
    return jax.shard_map(
        per_device,
        mesh=mesh,
        in_specs=(P(("parts", "col")), P(), P(), P(), P(), P(), P(), P("parts"), P(None, "col")),
        out_specs=(P(None, ("parts", "col")), P("parts", "col"), P(("parts", "col"))),
        check_vma=False,
    )
```

```python
import functools
import math

import jax
import jax.numpy as jnp
from jax import lax
from jax.experimental import pallas as pl
from jax.experimental.pallas import tpu as pltpu
from jax.sharding import PartitionSpec as P

STEPS = 3
LANES = 128
SINE = (3.1415926444, -5.1677100819, 2.5500775297, -0.5982913039, 0.0776576582)
VMEM = pl.BlockSpec(memory_space=pltpu.VMEM)
SMEM = pl.BlockSpec(memory_space=pltpu.SMEM)
ANY = pl.BlockSpec(memory_space=pl.ANY)


def params(mib):
    return pltpu.CompilerParams(vmem_limit_bytes=mib * 2**20)


def split(table, parts):
    out = []
    for _ in range(parts):
        piece = table.astype(jnp.bfloat16)
        out.append(piece)
        table = table - piece.astype(jnp.float32)
    return out


def lookup(pieces, index):
    rows = pieces[0].shape[1]
    n = index.shape[1]
    hot = lax.broadcasted_iota(jnp.int32, (rows, n), 0) == (index >> 7)
    hot = jnp.where(hot, 1.0, 0.0).astype(jnp.bfloat16)
    dims = (((1,), (0,)), ((), ()))
    total = sum(lax.dot_general(p, hot, dims, preferred_element_type=jnp.float32) for p in pieces)
    lane = lax.broadcasted_iota(jnp.int32, (LANES, n), 0) == (index & 127)
    return jnp.sum(jnp.where(lane, total, 0.0), axis=0, keepdims=True)


def newton(a_head, a_tail, self_head, cross, self_tail, bsus, hchg):
    inj_head = jnp.zeros_like(a_head)
    inj_tail = jnp.zeros_like(a_head)
    for step in range(1, STEPS + 1):
        level = step / STEPS
        end_head = a_head + self_head * inj_head + cross * inj_tail
        end_tail = a_tail + cross * inj_head + self_tail * inj_tail
        spread = end_head - end_tail
        sine_val = jnp.sin(spread)
        cosine_val = jnp.cos(spread)
        resid_head = inj_head - level * (bsus * sine_val + hchg * end_head)
        resid_tail = inj_tail - level * (-bsus * sine_val + hchg * end_tail)
        diag_term = bsus * cosine_val + hchg
        cross_term = -bsus * cosine_val
        jac_one = 1.0 - level * (diag_term * self_head + cross_term * cross)
        jac_two = -level * (diag_term * cross + cross_term * self_tail)
        jac_three = -level * (cross_term * self_head + diag_term * cross)
        jac_four = 1.0 - level * (cross_term * cross + diag_term * self_tail)
        determinant = jac_one * jac_four - jac_two * jac_three
        inj_head = inj_head - (jac_four * resid_head - jac_two * resid_tail) / determinant
        inj_tail = inj_tail - (jac_one * resid_tail - jac_three * resid_head) / determinant
    return inj_head, inj_tail


def addresses(row, width):
    return (row >> 3) * (8 * width) + (row & 7)


def stage(pairs, sem):
    copies = [pltpu.make_async_copy(src, dst, sem.at[i]) for i, (src, dst) in enumerate(pairs)]
    for copy in copies:
        copy.start()
    return copies


def ends_kernel(width, me_ref, ids_ref, from_ref, to_ref, slot_ref, sus_ref, chg_ref, base_ref, zinv_ref,
                state_ref, pick_ref, rows_h, rows_t, from_v, to_v, slot_v, sus_v, chg_v, base_v, zinv_v,
                ends_v, ends_s, sem):
    blocks = ids_ref.shape[0]
    first = me_ref[0] * width * LANES
    copies = stage([(from_ref, from_v), (to_ref, to_v), (slot_ref, slot_v), (sus_ref, sus_v),
                    (chg_ref, chg_v), (base_ref, base_v), (zinv_ref, zinv_v)], sem)
    for copy in copies[:-1]:
        copy.wait()
    f_parts = split(from_v[...].astype(jnp.float32).T, 2)
    t_parts = split(to_v[...].astype(jnp.float32).T, 2)
    s_parts = split(slot_v[...].astype(jnp.float32).T, 2)
    sus_parts = split(sus_v[...].T, 3)
    chg_parts = split(chg_v[...].T, 3)
    base_parts = split(base_v[...].T, 3)
    heads, tails = [], []
    for b in range(blocks):
        ids = ids_ref[b:b + 1, :]
        heads.append(lookup(s_parts, lookup(f_parts, ids).astype(jnp.int32)).astype(jnp.int32))
        tails.append(lookup(s_parts, lookup(t_parts, ids).astype(jnp.int32)).astype(jnp.int32))
        ends_v[b:b + 1, :] = addresses(heads[b], width)
        ends_v[blocks + b:blocks + b + 1, :] = addresses(tails[b], width)
    copy = pltpu.make_async_copy(ends_v, ends_s, sem.at[0])
    copy.start()
    for b in range(blocks):
        row = slice(b, b + 1)
        ids = ids_ref[row, :]
        state_ref[0, row, :] = lookup(base_parts, heads[b])
        state_ref[1, row, :] = lookup(base_parts, tails[b])
        state_ref[2, row, :] = lookup(sus_parts, ids)
        state_ref[3, row, :] = lookup(chg_parts, ids)
        state_ref[4, row, :] = (heads[b] - first).astype(jnp.float32)
        state_ref[5, row, :] = (tails[b] - first).astype(jnp.float32)
    copy.wait()
    copies[-1].wait()

    def block(b, carry):
        def fetch(g, carry):
            for i in range(16):
                o = g * 16 + i
                head = ends_s[b, o]
                tail = ends_s[blocks + b, o]
                for t in range(width):
                    rows_h[b, t, pl.ds(o, 1), :] = zinv_v[pl.ds(head + 8 * t, 1), :]
                    rows_t[b, t, pl.ds(o, 1), :] = zinv_v[pl.ds(tail + 8 * t, 1), :]
            return carry

        lax.fori_loop(0, LANES // 16, fetch, 0)
        square = (LANES, LANES)
        at_h = jnp.broadcast_to(state_ref[4, pl.ds(b, 1), :], square).T
        at_t = jnp.broadcast_to(state_ref[5, pl.ds(b, 1), :], square).T
        lane = lax.broadcasted_iota(jnp.int32, square, 1).astype(jnp.float32)
        hh = ht = tt = jnp.zeros(square, jnp.float32)
        for t in range(width):
            is_h = at_h == lane + float(t * LANES)
            is_t = at_t == lane + float(t * LANES)
            hh = jnp.where(is_h, rows_h[b, t], hh)
            ht = jnp.where(is_t, rows_h[b, t], ht)
            tt = jnp.where(is_t, rows_t[b, t], tt)
        for i, pick in enumerate((hh, ht, tt)):
            pick_ref[pl.ds(i * blocks + b, 1), :] = jnp.sum(pick.T, axis=0, keepdims=True)
        return carry

    lax.fori_loop(0, blocks, block, 0)


def spread_kernel(me_ref, state_ref, pick_ref, base_ref, rows_h, rows_t, inj_ref, dev_ref, *units):
    blocks, width = rows_h.shape[:2]
    me = me_ref[0]
    inj_h, inj_t = newton(state_ref[0], state_ref[1], pick_ref[:blocks], pick_ref[blocks:2 * blocks],
                          pick_ref[2 * blocks:], state_ref[2], state_ref[3])
    inj_ref[0] = inj_h
    inj_ref[1] = inj_t
    for d, unit in enumerate(units):
        blk = (me >> 1) ^ d
        scale_h = jnp.broadcast_to(inj_ref[0, pl.ds(blk, 1), :], (LANES, LANES)).T
        scale_t = jnp.broadcast_to(inj_ref[1, pl.ds(blk, 1), :], (LANES, LANES)).T
        for t in range(width):
            at = slice(t * LANES, (t + 1) * LANES)
            dev = scale_h * rows_h[blk, t] + scale_t * rows_t[blk, t]
            dev_ref[pl.ds(pl.multiple_of(blk * LANES, LANES), LANES), at] = dev
            angle = base_ref[pl.ds(me * width + t, 1), :] + dev
            unit[at, :] = (angle * (1.0 / math.pi)).T


def prep_kernel(me_ref, from_ref, to_ref, slot_ref, sus_ref, rate_ref, f_ref, t_ref, ratio_ref):
    half = f_ref.shape[0]
    me = me_ref[0]
    start = (me & 1) * half
    flip = me * (slot_ref.shape[0] * LANES // me_ref[1])
    s_parts = split(slot_ref[...].astype(jnp.float32).T, 2)

    def group(g, carry):
        for i in range(8):
            row = pl.ds(start + g * 8 + i, 1)
            out = pl.ds(g * 8 + i, 1)
            f_ref[out, :] = lookup(s_parts, from_ref[row, :]).astype(jnp.int32) ^ flip
            t_ref[out, :] = lookup(s_parts, to_ref[row, :]).astype(jnp.int32) ^ flip
            ratio_ref[out, :] = sus_ref[row, :] / rate_ref[row, :]
        return carry

    lax.fori_loop(0, half // 8, group, 0)


def worst_kernel(me_ref, f_s, t_s, ratio_ref, ids_ref, *rest):
    pieces, (out_ref, table, diff, best, sem) = rest[:-5], rest[-5:]
    unit = pieces[0].shape[0]
    copies = []
    for i, piece in enumerate(pieces):
        copy = pltpu.make_async_copy(piece, table.at[pl.ds(i * unit, unit)], sem.at[i])
        copy.start()
        copies.append(copy)
    for copy in copies:
        copy.wait()
    half = f_s.shape[0]
    me = me_ref[0]
    ids = ids_ref[pl.ds(me >> 1, 1), :]
    start = (me & 1) * half
    best[...] = jnp.zeros_like(best)

    def block(b, carry):
        for j in range(LANES):
            diff[pl.ds(j, 1), :] = table[pl.ds(f_s[b, j], 1), :] - table[pl.ds(t_s[b, j], 1), :]
        turn = diff[...]
        turn = turn - jnp.round(turn)
        square = turn * turn
        poly = SINE[4]
        for c in SINE[3::-1]:
            poly = poly * square + c
        ratio = jnp.broadcast_to(ratio_ref[pl.ds(b, 1), :], (LANES, LANES)).T
        load = jnp.abs(turn * poly) * ratio
        branch = lax.broadcasted_iota(jnp.int32, (LANES, LANES), 0) + (start + b) * LANES
        load = jnp.where(branch == ids, 0.0, load)
        best[...] = jnp.maximum(best[...], jnp.max(load.reshape(LANES // 8, 8, LANES), axis=0))
        return carry

    lax.fori_loop(0, half, block, 0)
    out_ref[...] = jnp.max(best[...], axis=0, keepdims=True)


def per_device(
    outages, branch_from, branch_to, bus_slot, susceptance, charging, rating, base_angles, zinv
):
    n_col = lax.axis_size("col")
    buses, cols = zinv.shape
    own = outages.shape[0]
    total = own * n_col
    blocks = total // LANES
    chips = n_col // 2
    assert own * 2 == LANES and chips & (chips - 1) == 0
    me = lax.axis_index("col")
    where = jnp.stack([me, jnp.int32(n_col)])
    tab = lambda a: a.reshape(-1, LANES)
    from2, to2, slot2, sus2, chg2, rate2, base2 = map(
        tab, (branch_from, branch_to, bus_slot, susceptance, charging, rating, base_angles)
    )
    i32 = lambda *s: jax.ShapeDtypeStruct(s, jnp.int32)
    f32 = lambda *s: jax.ShapeDtypeStruct(s, jnp.float32)

    flat = zinv.reshape(buses // 8, 8, cols // LANES, LANES).transpose(0, 2, 1, 3).reshape(-1, LANES)
    ids = lax.dynamic_update_slice(jnp.zeros((total,), jnp.int32), outages, (me * own,))
    ids = lax.psum(tab(ids), "col")

    width = cols // LANES
    like = lambda a: pltpu.VMEM(a.shape, a.dtype)
    state, picks, rows_h, rows_t = pl.pallas_call(
        functools.partial(ends_kernel, width),
        name="ends",
        out_shape=[f32(6, blocks, LANES), f32(3 * blocks, LANES)] + [f32(blocks, width, LANES, LANES)] * 2,
        in_specs=[SMEM, VMEM] + [ANY] * 7,
        out_specs=[VMEM] * 4,
        scratch_shapes=[like(from2), like(to2), like(slot2), like(sus2), like(chg2), like(base2), like(flat),
                        pltpu.VMEM((2 * blocks, LANES), jnp.int32), pltpu.SMEM((2 * blocks, LANES), jnp.int32),
                        pltpu.SemaphoreType.DMA((7,))],
        compiler_params=params(48),
    )(where, ids, from2, to2, slot2, sus2, chg2, base2, flat)

    swap = lambda a, m: lax.ppermute(a, "col", [(i, i ^ m) for i in range(n_col)])
    step = 1
    while step < n_col:
        picks = sum([swap(picks, m * step) for m in range(1, min(4, n_col // step))], picks)
        step *= 4

    injections, deviation, *units = pl.pallas_call(
        spread_kernel,
        name="spread",
        out_shape=[f32(2, blocks, LANES), f32(total, cols)] + [f32(cols, LANES)] * chips,
        in_specs=[SMEM] + [VMEM] * 5,
        out_specs=[VMEM] * (2 + chips),
        compiler_params=params(32),
    )(where, state, picks, base2, rows_h, rows_t)

    half = from2.shape[0] // 2
    f_rel, t_rel, ratio = pl.pallas_call(
        prep_kernel,
        name="prep",
        out_shape=[i32(half, LANES), i32(half, LANES), f32(half, LANES)],
        in_specs=[SMEM] + [VMEM] * 5,
        out_specs=[VMEM] * 3,
        cost_estimate=pl.CostEstimate(flops=10**9, bytes_accessed=10**6, transcendentals=0),
    )(where, from2, to2, slot2, sus2, rate2)

    far = sorted(range(1, chips), reverse=True)
    got = {0: units[0]}
    for d in far:
        got[d] = swap(units[d], 2 * d)
    pieces = []
    for d in range(chips):
        pieces.append(got[d])
        pieces.append(swap(got[d], 1))

    worst = pl.pallas_call(
        worst_kernel,
        name="worst",
        out_shape=f32(1, LANES),
        in_specs=[SMEM] * 3 + [VMEM] * 2 + [ANY] * n_col,
        out_specs=VMEM,
        scratch_shapes=[pltpu.VMEM((buses, LANES), jnp.float32), pltpu.VMEM((LANES, LANES), jnp.float32),
                        pltpu.VMEM((8, LANES), jnp.float32), pltpu.SemaphoreType.DMA((n_col,))],
        compiler_params=params(16),
    )(where, f_rel, t_rel, ratio, ids, *pieces)
    other = swap(worst, 1)
    worst = lax.dynamic_slice(jnp.maximum(worst, other)[0], ((me & 1) * own,), (own,))
    inj = lax.dynamic_slice(injections.reshape(2, total), (0, me * own), (2, own))
    return inj, deviation, worst


def solution(mesh):
    return jax.shard_map(
        per_device,
        mesh=mesh,
        in_specs=(P(("parts", "col")), P(), P(), P(), P(), P(), P(), P("parts"), P(None, "col")),
        out_specs=(P(None, ("parts", "col")), P("parts", "col"), P(("parts", "col"))),
        check_vma=False,
    )
```

```python
import functools
import math

import jax
import jax.numpy as jnp
from jax import lax
from jax.experimental import pallas as pl
from jax.experimental.pallas import tpu as pltpu
from jax.sharding import PartitionSpec as P

STEPS = 3
LANES = 128
GROUP = 4
SINE = (3.1415926444, -5.1677100819, 2.5500775297, -0.5982913039, 0.0776576582)
VMEM = pl.BlockSpec(memory_space=pltpu.VMEM)
SMEM = pl.BlockSpec(memory_space=pltpu.SMEM)
ANY = pl.BlockSpec(memory_space=pl.ANY)
HBM = pl.BlockSpec(memory_space=pltpu.HBM)


def cost(micros):
    return pl.CostEstimate(flops=micros * 10**9, bytes_accessed=10**6, transcendentals=0)


def params(mib):
    return pltpu.CompilerParams(vmem_limit_bytes=mib * 2**20)


def split(table, parts):
    out = []
    for _ in range(parts):
        piece = table.astype(jnp.bfloat16)
        out.append(piece)
        table = table - piece.astype(jnp.float32)
    return out


def lookup(pieces, index):
    rows = pieces[0].shape[1]
    n = index.shape[1]
    hot = lax.broadcasted_iota(jnp.int32, (rows, n), 0) == (index >> 7)
    hot = jnp.where(hot, 1.0, 0.0).astype(jnp.bfloat16)
    dims = (((1,), (0,)), ((), ()))
    total = sum(lax.dot_general(p, hot, dims, preferred_element_type=jnp.float32) for p in pieces)
    lane = lax.broadcasted_iota(jnp.int32, (LANES, n), 0) == (index & 127)
    return jnp.sum(jnp.where(lane, total, 0.0), axis=0, keepdims=True)


def newton(a_head, a_tail, self_head, cross, self_tail, bsus, hchg):
    inj_head = jnp.zeros_like(a_head)
    inj_tail = jnp.zeros_like(a_head)
    for step in range(1, STEPS + 1):
        level = step / STEPS
        end_head = a_head + self_head * inj_head + cross * inj_tail
        end_tail = a_tail + cross * inj_head + self_tail * inj_tail
        spread = end_head - end_tail
        sine_val = jnp.sin(spread)
        cosine_val = jnp.cos(spread)
        resid_head = inj_head - level * (bsus * sine_val + hchg * end_head)
        resid_tail = inj_tail - level * (-bsus * sine_val + hchg * end_tail)
        diag_term = bsus * cosine_val + hchg
        cross_term = -bsus * cosine_val
        jac_one = 1.0 - level * (diag_term * self_head + cross_term * cross)
        jac_two = -level * (diag_term * cross + cross_term * self_tail)
        jac_three = -level * (cross_term * self_head + diag_term * cross)
        jac_four = 1.0 - level * (cross_term * cross + diag_term * self_tail)
        determinant = jac_one * jac_four - jac_two * jac_three
        inj_head = inj_head - (jac_four * resid_head - jac_two * resid_tail) / determinant
        inj_tail = inj_tail - (jac_one * resid_tail - jac_three * resid_head) / determinant
    return inj_head, inj_tail


def addresses(row, width):
    return (row >> 3) * (8 * width) + (row & 7)


def stage(pairs, sem):
    copies = [pltpu.make_async_copy(src, dst, sem.at[i]) for i, (src, dst) in enumerate(pairs)]
    for copy in copies:
        copy.start()
    return copies


def ends_kernel(width, me_ref, ids_ref, from_ref, to_ref, slot_ref, sus_ref, chg_ref, base_ref, zinv_ref,
                state_ref, pick_ref, rows_h, rows_t, from_v, to_v, slot_v, sus_v, chg_v, base_v, zinv_v,
                ends_v, ends_s, sem):
    blocks = ids_ref.shape[0]
    first = me_ref[0] * width * LANES
    copies = stage([(from_ref, from_v), (to_ref, to_v), (slot_ref, slot_v), (sus_ref, sus_v),
                    (chg_ref, chg_v), (base_ref, base_v), (zinv_ref, zinv_v)], sem)
    for copy in copies[:-1]:
        copy.wait()
    f_parts = split(from_v[...].astype(jnp.float32).T, 2)
    t_parts = split(to_v[...].astype(jnp.float32).T, 2)
    s_parts = split(slot_v[...].astype(jnp.float32).T, 2)
    sus_parts = split(sus_v[...].T, 3)
    chg_parts = split(chg_v[...].T, 3)
    base_parts = split(base_v[...].T, 3)
    heads, tails = [], []
    for b in range(blocks):
        ids = ids_ref[b:b + 1, :]
        heads.append(lookup(s_parts, lookup(f_parts, ids).astype(jnp.int32)).astype(jnp.int32))
        tails.append(lookup(s_parts, lookup(t_parts, ids).astype(jnp.int32)).astype(jnp.int32))
        ends_v[b:b + 1, :] = addresses(heads[b], width)
        ends_v[blocks + b:blocks + b + 1, :] = addresses(tails[b], width)
    copy = pltpu.make_async_copy(ends_v, ends_s, sem.at[0])
    copy.start()
    for b in range(blocks):
        row = slice(b, b + 1)
        ids = ids_ref[row, :]
        state_ref[0, row, :] = lookup(base_parts, heads[b])
        state_ref[1, row, :] = lookup(base_parts, tails[b])
        state_ref[2, row, :] = lookup(sus_parts, ids)
        state_ref[3, row, :] = lookup(chg_parts, ids)
        state_ref[4, row, :] = (heads[b] - first).astype(jnp.float32)
        state_ref[5, row, :] = (tails[b] - first).astype(jnp.float32)
    copy.wait()
    copies[-1].wait()

    def block(b, carry):
        def fetch(g, carry):
            for i in range(16):
                o = g * 16 + i
                head = ends_s[b, o]
                tail = ends_s[blocks + b, o]
                for t in range(width):
                    rows_h[b, t, pl.ds(o, 1), :] = zinv_v[pl.ds(head + 8 * t, 1), :]
                    rows_t[b, t, pl.ds(o, 1), :] = zinv_v[pl.ds(tail + 8 * t, 1), :]
            return carry

        lax.fori_loop(0, LANES // 16, fetch, 0)
        square = (LANES, LANES)
        at_h = jnp.broadcast_to(state_ref[4, pl.ds(b, 1), :], square).T
        at_t = jnp.broadcast_to(state_ref[5, pl.ds(b, 1), :], square).T
        lane = lax.broadcasted_iota(jnp.int32, square, 1).astype(jnp.float32)
        hh = ht = tt = jnp.zeros(square, jnp.float32)
        for t in range(width):
            is_h = at_h == lane + float(t * LANES)
            is_t = at_t == lane + float(t * LANES)
            hh = jnp.where(is_h, rows_h[b, t], hh)
            ht = jnp.where(is_t, rows_h[b, t], ht)
            tt = jnp.where(is_t, rows_t[b, t], tt)
        for i, pick in enumerate((hh, ht, tt)):
            pick_ref[pl.ds(i * blocks + b, 1), :] = jnp.sum(pick.T, axis=0, keepdims=True)
        return carry

    lax.fori_loop(0, blocks, block, 0)


def spread_kernel(me_ref, state_ref, pick_ref, base_ref, rows_h, rows_t, inj_ref, dev_ref, *units):
    blocks, width = rows_h.shape[:2]
    me = me_ref[0]
    inj_h, inj_t = newton(state_ref[0], state_ref[1], pick_ref[:blocks], pick_ref[blocks:2 * blocks],
                          pick_ref[2 * blocks:], state_ref[2], state_ref[3])
    inj_ref[0] = inj_h
    inj_ref[1] = inj_t
    for d, unit in enumerate(units):
        blk = (me >> 1) ^ d
        scale_h = jnp.broadcast_to(inj_ref[0, pl.ds(blk, 1), :], (LANES, LANES)).T
        scale_t = jnp.broadcast_to(inj_ref[1, pl.ds(blk, 1), :], (LANES, LANES)).T
        for t in range(width):
            at = slice(t * LANES, (t + 1) * LANES)
            dev = scale_h * rows_h[blk, t] + scale_t * rows_t[blk, t]
            dev_ref[pl.ds(pl.multiple_of(blk * LANES, LANES), LANES), at] = dev
            angle = base_ref[pl.ds(me * width + t, 1), :] + dev
            unit[at, :] = (angle * (1.0 / math.pi)).T


def prep_kernel(unit, mid, last, me_ref, from_ref, to_ref, slot_ref, sus_ref, rate_ref,
                f_ref, t_ref, ratio_ref, k_ref, cnt_ref, from_v, to_v, slot_v, sus_v, rate_v, sem):
    copies = stage([(from_ref, from_v), (to_ref, to_v), (slot_ref, slot_v), (sus_ref, sus_v),
                    (rate_ref, rate_v)], sem)
    for copy in copies:
        copy.wait()
    half = f_ref.shape[0]
    me = me_ref[0]
    start = (me & 1) * half
    flip = me * unit
    shift = (2 * unit).bit_length() - 1
    s_parts = split(slot_v[...].astype(jnp.float32).T, 2)
    square = (LANES, LANES)
    before = lax.broadcasted_iota(jnp.int32, square, 0) < lax.broadcasted_iota(jnp.int32, square, 1)
    before = jnp.where(before, 1.0, 0.0).astype(jnp.bfloat16)
    lane = lax.broadcasted_iota(jnp.int32, (1, LANES), 1).astype(jnp.float32)
    slots = lax.broadcasted_iota(jnp.int32, (GROUP * LANES, LANES), 0).astype(jnp.float32)

    def group(g, carry):
        fs, ts, ratios, first, second = [], [], [], [], []
        for i in range(GROUP):
            row = pl.ds(start + g * GROUP + i, 1)
            f = lookup(s_parts, from_v[row, :]).astype(jnp.int32) ^ flip
            t = lookup(s_parts, to_v[row, :]).astype(jnp.int32) ^ flip
            fs.append(f)
            ts.append(t)
            ratios.append(sus_v[row, :] / rate_v[row, :])
            f_chip, t_chip = f >> shift, t >> shift
            late = (f_chip == last) | (t_chip == last)
            middle = ((f_chip == mid) | (t_chip == mid)) & jnp.logical_not(late)
            first.append(jnp.where(late | middle, 0.0, 1.0))
            second.append(jnp.where(middle, 1.0, 0.0))
        flags = jnp.concatenate(first + second, 0)
        ahead = jnp.dot(flags.astype(jnp.bfloat16), before, preferred_element_type=jnp.float32)
        sums = jnp.sum(flags, axis=1, keepdims=True)
        n_first = sum(sums[i:i + 1] for i in range(GROUP))
        n_second = sum(sums[GROUP + i:GROUP + i + 1] for i in range(GROUP))
        off_first = off_second = jnp.zeros((1, 1), jnp.float32)
        total = jnp.zeros((16, GROUP * LANES), jnp.float32)
        for i in range(GROUP):
            c_first = off_first + ahead[i:i + 1]
            c_second = off_second + ahead[GROUP + i:GROUP + i + 1]
            rest = n_first + n_second + (lane + float(i * LANES)) - c_first - c_second
            place = jnp.where(first[i] > 0.5, c_first, jnp.where(second[i] > 0.5, n_first + c_second, rest))
            off_first = off_first + sums[i:i + 1]
            off_second = off_second + sums[GROUP + i:GROUP + i + 1]
            hot = jnp.where(slots == place, 1.0, 0.0).astype(jnp.bfloat16)
            high, low = fs[i] >> 7, fs[i] & 127
            rows = [high, low, ts[i] >> 7, ts[i] & 127]
            rows = [r.astype(jnp.float32) for r in rows]
            rows += [p.astype(jnp.float32) for p in split(ratios[i], 3)]
            rows += [jnp.full((1, LANES), float(i)), lane] + [jnp.zeros((1, LANES), jnp.float32)] * 7
            values = jnp.concatenate(rows, 0).astype(jnp.bfloat16)
            total += lax.dot_general(values, hot, (((1,), (1,)), ((), ())), preferred_element_type=jnp.float32)
        for i in range(GROUP):
            out = pl.ds(g * GROUP + i, 1)
            part = total[:, i * LANES:(i + 1) * LANES]
            f_ref[out, :] = (part[0:1] * 128.0 + part[1:2]).astype(jnp.int32)
            t_ref[out, :] = (part[2:3] * 128.0 + part[3:4]).astype(jnp.int32)
            ratio_ref[out, :] = part[4:5] + part[5:6] + part[6:7]
            origin = ((start + g * GROUP) * LANES).astype(jnp.float32)
            k_ref[out, :] = part[7:8] * 128.0 + part[8:9] + origin
        wide = lambda a: jnp.broadcast_to(a, (1, LANES)).astype(jnp.int32) >> 7
        cnt_ref[0, pl.ds(g, 1), :] = wide(n_first)
        cnt_ref[1, pl.ds(g, 1), :] = wide(n_first + n_second)
        return carry

    lax.fori_loop(0, half // GROUP, group, 0)


def gate_kernel(*refs):
    pass


def gate(value, *after):
    return pl.pallas_call(
        gate_kernel,
        name="gate",
        out_shape=jax.ShapeDtypeStruct(value.shape, value.dtype),
        in_specs=[ANY] * (1 + len(after)),
        out_specs=ANY,
        input_output_aliases={0: 0},
    )(value, *after)


def worst_kernel(level, places, me_ref, f_ref, t_ref, cnt_ref, ratio_ref, k_ref, ids_ref, *rest):
    if level:
        best_in, _, *rest = rest
    n = len(places)
    pieces, (best, table, f_s, t_s, cnt_s, diff, sem) = rest[:n], rest[n:]
    pairs = [(f_ref, f_s), (t_ref, t_s), (cnt_ref, cnt_s)]
    pairs += [(p, table.at[pl.ds(i * p.shape[0], p.shape[0])]) for p, i in zip(pieces, places)]
    copies = stage(pairs, sem)
    half = f_ref.shape[0]
    ids = ids_ref[pl.ds(me_ref[0] >> 1, 1), :].astype(jnp.float32)
    best[...] = best_in[...] if level else jnp.zeros_like(best)
    for copy in copies:
        copy.wait()

    def block(b, carry):
        for j in range(LANES):
            diff[pl.ds(j, 1), :] = table[pl.ds(f_s[b, j], 1), :] - table[pl.ds(t_s[b, j], 1), :]
        turn = diff[...]
        turn = turn - jnp.round(turn)
        square = turn * turn
        poly = SINE[4]
        for c in SINE[3::-1]:
            poly = poly * square + c
        ratio = jnp.broadcast_to(ratio_ref[pl.ds(b, 1), :], (LANES, LANES)).T
        branch = jnp.broadcast_to(k_ref[pl.ds(b, 1), :], (LANES, LANES)).T
        load = jnp.where(branch == ids, 0.0, jnp.abs(turn * poly) * ratio)
        best[...] = jnp.maximum(best[...], jnp.max(load.reshape(LANES // 8, 8, LANES), axis=0))
        return carry

    def group(g, carry):
        low = 0 if level == 0 else cnt_s[level - 1, g, 0]
        high = GROUP if level == 2 else cnt_s[level, g, 0]
        return lax.fori_loop(g * GROUP + low, g * GROUP + high, block, carry)

    lax.fori_loop(0, half // GROUP, group, 0)
    if level == 2:
        best[...] = jnp.broadcast_to(jnp.max(best[...], axis=0, keepdims=True), best.shape)


def per_device(
    outages, branch_from, branch_to, bus_slot, susceptance, charging, rating, base_angles, zinv
):
    n_col = lax.axis_size("col")
    buses, cols = zinv.shape
    own = outages.shape[0]
    total = own * n_col
    blocks = total // LANES
    chips = n_col // 2
    assert own * 2 == LANES and chips & (chips - 1) == 0
    me = lax.axis_index("col")
    where = jnp.stack([me, jnp.int32(n_col)])
    tab = lambda a: a.reshape(-1, LANES)
    from2, to2, slot2, sus2, chg2, rate2, base2 = map(
        tab, (branch_from, branch_to, bus_slot, susceptance, charging, rating, base_angles)
    )
    i32 = lambda *s: jax.ShapeDtypeStruct(s, jnp.int32)
    f32 = lambda *s: jax.ShapeDtypeStruct(s, jnp.float32)

    flat = zinv.reshape(buses // 8, 8, cols // LANES, LANES).transpose(0, 2, 1, 3).reshape(-1, LANES)
    ids = lax.dynamic_update_slice(jnp.zeros((total,), jnp.int32), outages, (me * own,))
    ids = lax.psum(tab(ids), "col")

    width = cols // LANES
    like = lambda a: pltpu.VMEM(a.shape, a.dtype)
    state, picks, rows_h, rows_t = pl.pallas_call(
        functools.partial(ends_kernel, width),
        name="ends",
        out_shape=[f32(6, blocks, LANES), f32(3 * blocks, LANES)] + [f32(blocks, width, LANES, LANES)] * 2,
        in_specs=[SMEM, VMEM] + [HBM] * 7,
        out_specs=[VMEM] * 4,
        scratch_shapes=[like(from2), like(to2), like(slot2), like(sus2), like(chg2), like(base2), like(flat),
                        pltpu.VMEM((2 * blocks, LANES), jnp.int32), pltpu.SMEM((2 * blocks, LANES), jnp.int32),
                        pltpu.SemaphoreType.DMA((7,))],
        compiler_params=params(48),
    )(where, ids, from2, to2, slot2, sus2, chg2, base2, flat)

    swap = lambda a, m: lax.ppermute(a, "col", [(i, i ^ m) for i in range(n_col)])
    step = 1
    while step < n_col:
        picks = sum([swap(picks, m * step) for m in range(1, min(4, n_col // step))], picks)
        step *= 4

    injections, deviation, *units = pl.pallas_call(
        spread_kernel,
        name="spread",
        out_shape=[f32(2, blocks, LANES), f32(total, cols)] + [f32(cols, LANES)] * chips,
        in_specs=[SMEM] + [VMEM] * 5,
        out_specs=[VMEM] * (2 + chips),
        compiler_params=params(32),
    )(where, state, picks, base2, rows_h, rows_t)

    half = from2.shape[0] // 2
    near = list(range(1, chips // 2))
    *far, mid, last = range(chips // 2, chips)
    f_rel, t_rel, ratio, k_rel, counts = pl.pallas_call(
        functools.partial(prep_kernel, cols, mid, last),
        name="prep",
        out_shape=[i32(half, LANES), i32(half, LANES), f32(half, LANES), f32(half, LANES),
                   i32(2, half // GROUP, LANES)],
        in_specs=[SMEM] + [HBM] * 5,
        out_specs=[VMEM] * 5,
        scratch_shapes=[like(from2), like(to2), like(slot2), like(sus2), like(rate2),
                        pltpu.SemaphoreType.DMA((5,))],
        compiler_params=params(16),
        cost_estimate=cost(12),
    )(where, from2, to2, slot2, sus2, rate2)

    got = {0: units[0]}
    for d in far + near:
        got[d] = swap(units[d], 2 * d)
    between = swap(gate(units[mid], got[far[0]], counts), 2 * mid)
    arrived = swap(gate(units[last], got[far[-1]]), 2 * last)

    def worst_stage(level, ds, *carried):
        places = [2 * d + e for d in ds for e in (0, 1)]
        pieces = [p for d in ds for p in (got[d], swap(got[d], 1))]
        return pl.pallas_call(
            functools.partial(worst_kernel, level, places),
            name=f"worst{level}",
            out_shape=[f32(8, LANES), f32(buses, LANES)],
            in_specs=[SMEM] + [HBM] * 3 + [VMEM] * (3 + len(carried)) + [ANY] * len(pieces),
            out_specs=[VMEM] * 2,
            scratch_shapes=[pltpu.SMEM(f_rel.shape, jnp.int32), pltpu.SMEM(t_rel.shape, jnp.int32),
                            pltpu.SMEM(counts.shape, jnp.int32), pltpu.VMEM((LANES, LANES), jnp.float32),
                            pltpu.SemaphoreType.DMA((3 + len(pieces),))],
            input_output_aliases={7 + i: i for i in range(len(carried))},
            compiler_params=params(16),
            cost_estimate=cost((9, 4, 4)[level]),
        )(where, f_rel, t_rel, counts, ratio, k_rel, ids, *carried, *pieces)

    best, table = worst_stage(0, [0] + near + far)
    got[mid] = gate(between, best)
    best, table = worst_stage(1, [mid], best, table)
    got[last] = gate(arrived, best)
    best, _ = worst_stage(2, [last], best, table)
    worst = lax.slice(best, (0, 0), (1, LANES))
    worst = lax.dynamic_slice(jnp.maximum(worst, swap(worst, 1))[0], ((me & 1) * own,), (own,))
    inj = lax.dynamic_slice(injections.reshape(2, total), (0, me * own), (2, own))
    return inj, deviation, worst


def solution(mesh):
    return jax.shard_map(
        per_device,
        mesh=mesh,
        in_specs=(P(("parts", "col")), P(), P(), P(), P(), P(), P(), P("parts"), P(None, "col")),
        out_specs=(P(None, ("parts", "col")), P("parts", "col"), P(("parts", "col"))),
        check_vma=False,
    )
```

```python
import functools
import math

import jax
import jax.numpy as jnp
from jax import lax
from jax.experimental import pallas as pl
from jax.experimental.pallas import tpu as pltpu
from jax.sharding import PartitionSpec as P

STEPS = 3
LANES = 128
GROUP = 4
SINE = (3.1415926444, -5.1677100819, 2.5500775297, -0.5982913039, 0.0776576582)
VMEM = pl.BlockSpec(memory_space=pltpu.VMEM)
SMEM = pl.BlockSpec(memory_space=pltpu.SMEM)
ANY = pl.BlockSpec(memory_space=pl.ANY)


def params(mib):
    return pltpu.CompilerParams(vmem_limit_bytes=mib * 2**20)


def split(table, parts):
    out = []
    for _ in range(parts):
        piece = table.astype(jnp.bfloat16)
        out.append(piece)
        table = table - piece.astype(jnp.float32)
    return out


def columns(tables):
    return jnp.concatenate([jnp.concatenate(split(t.T, 3), 1) for t in tables], 0)


def lookup(turned, index):
    rows = turned.shape[1] // 3
    n = index.shape[1]
    hot = lax.broadcasted_iota(jnp.int32, (rows, n), 0) == (index >> 7)
    hot = jnp.where(hot, 1.0, 0.0).astype(jnp.bfloat16)
    picked = jnp.dot(turned, jnp.concatenate([hot] * 3, 0), preferred_element_type=jnp.float32)
    lane = lax.broadcasted_iota(jnp.int32, (LANES, n), 0) == (index & 127)
    return [jnp.sum(jnp.where(lane, picked[i:i + LANES], 0.0), axis=0, keepdims=True)
            for i in range(0, turned.shape[0], LANES)]


def newton(a_head, a_tail, self_head, cross, self_tail, bsus, hchg):
    inj_head = jnp.zeros_like(a_head)
    inj_tail = jnp.zeros_like(a_head)
    for step in range(1, STEPS + 1):
        level = step / STEPS
        end_head = a_head + self_head * inj_head + cross * inj_tail
        end_tail = a_tail + cross * inj_head + self_tail * inj_tail
        spread = end_head - end_tail
        sine_val = jnp.sin(spread)
        cosine_val = jnp.cos(spread)
        resid_head = inj_head - level * (bsus * sine_val + hchg * end_head)
        resid_tail = inj_tail - level * (-bsus * sine_val + hchg * end_tail)
        diag_term = bsus * cosine_val + hchg
        cross_term = -bsus * cosine_val
        jac_one = 1.0 - level * (diag_term * self_head + cross_term * cross)
        jac_two = -level * (diag_term * cross + cross_term * self_tail)
        jac_three = -level * (cross_term * self_head + diag_term * cross)
        jac_four = 1.0 - level * (cross_term * cross + diag_term * self_tail)
        determinant = jac_one * jac_four - jac_two * jac_three
        inj_head = inj_head - (jac_four * resid_head - jac_two * resid_tail) / determinant
        inj_tail = inj_tail - (jac_one * resid_tail - jac_three * resid_head) / determinant
    return inj_head, inj_tail


def addresses(row, width):
    return (row >> 3) * (8 * width) + (row & 7)


def stage(pairs, sem):
    copies = [pltpu.make_async_copy(src, dst, sem.at[i]) for i, (src, dst) in enumerate(pairs)]
    for copy in copies:
        copy.start()
    return copies


def ends_kernel(width, me_ref, ids_ref, from_ref, to_ref, slot_ref, sus_ref, chg_ref, base_ref, zinv_ref,
                state_ref, pick_ref, own_base_ref, rows_ref, from_v, to_v, slot_v, sus_v, chg_v, base_v,
                zinv_v, ends_v, ends_s, rows, sem, out_sem):
    total = ids_ref.shape[1]
    blocks = total // LANES
    first = me_ref[0] * width * LANES
    copies = stage([(from_ref, from_v), (to_ref, to_v), (slot_ref, slot_v), (sus_ref, sus_v),
                    (chg_ref, chg_v), (base_ref, base_v), (zinv_ref, zinv_v)], sem)
    for copy in copies[:-1]:
        copy.wait()
    branch = columns([from_v[...].astype(jnp.float32), to_v[...].astype(jnp.float32), sus_v[...], chg_v[...]])
    slot = columns([slot_v[...].astype(jnp.float32)])
    base = columns([base_v[...]])
    wide = min(total, 8 * LANES)
    for c in range(0, total, wide):
        ids = ids_ref[:, c:c + wide]
        f, t, sus, chg = lookup(branch, ids)
        ends, = lookup(slot, jnp.concatenate([f, t], 1).astype(jnp.int32))
        ends = ends.astype(jnp.int32)
        angle, = lookup(base, ends)
        place = addresses(ends, width)
        local = (ends - first).astype(jnp.float32)
        known = (angle[:, :wide], angle[:, wide:], sus, chg, local[:, :wide], local[:, wide:],
                 ids.astype(jnp.float32))
        for b in range(wide // LANES):
            row = slice(c // LANES + b, c // LANES + b + 1)
            at = slice(b * LANES, (b + 1) * LANES)
            ends_v[row, :] = place[:, at]
            ends_v[slice(blocks + row.start, blocks + row.stop), :] = place[:, b * LANES + wide:(b + 1) * LANES + wide]
            for i, value in enumerate(known):
                state_ref[i, row, :] = value[:, at]
    copy = pltpu.make_async_copy(ends_v, ends_s, sem.at[0])
    copy.start()
    for t in range(width):
        own_base_ref[t:t + 1, :] = base_v[pl.ds(me_ref[0] * width + t, 1), :]
    copy.wait()
    copies[-1].wait()

    def block(b, slot):
        def fetch(g, carry):
            for i in range(32):
                o = g * 32 + i
                head = ends_s[b, o]
                tail = ends_s[blocks + b, o]
                for t in range(width):
                    rows[slot, 0, t, pl.ds(o, 1), :] = zinv_v[pl.ds(head + 8 * t, 1), :]
                    rows[slot, 1, t, pl.ds(o, 1), :] = zinv_v[pl.ds(tail + 8 * t, 1), :]
            return carry

        lax.fori_loop(0, LANES // 32, fetch, 0)
        pltpu.make_async_copy(rows.at[slot], rows_ref.at[b], out_sem.at[slot]).start()
        square = (LANES, LANES)
        at_h = jnp.broadcast_to(state_ref[4, pl.ds(b, 1), :], square).T
        at_t = jnp.broadcast_to(state_ref[5, pl.ds(b, 1), :], square).T
        lane = lax.broadcasted_iota(jnp.int32, square, 1).astype(jnp.float32)
        hh = ht = tt = jnp.zeros(square, jnp.float32)
        for t in range(width):
            is_h = at_h == lane + float(t * LANES)
            is_t = at_t == lane + float(t * LANES)
            hh = jnp.where(is_h, rows[slot, 0, t], hh)
            ht = jnp.where(is_t, rows[slot, 0, t], ht)
            tt = jnp.where(is_t, rows[slot, 1, t], tt)
        for i, pick in enumerate((hh, ht, tt)):
            pick_ref[pl.ds(i * blocks + b, 1), :] = jnp.sum(pick.T, axis=0, keepdims=True)

    def pair(i, carry):
        for slot in (0, 1):
            @pl.when(i > 0)
            def _():
                pltpu.make_async_copy(rows.at[slot], rows_ref.at[2 * i - 2 + slot], out_sem.at[slot]).wait()

            block(2 * i + slot, slot)
        return carry

    lax.fori_loop(0, blocks // 2, pair, 0)
    for slot in (0, 1):
        pltpu.make_async_copy(rows.at[slot], rows_ref.at[blocks - 2 + slot], out_sem.at[slot]).wait()


def spread_kernel(chips, me_ref, state_ref, pick_ref, base_ref, rows_ref, inj_ref, dev_ref, *rest):
    units, (state, pick, base, inj, rows, dev, unit, in_sem, row_sem, out_sem) = rest[:chips], rest[chips:]
    blocks, _, width = rows.shape[:3]
    me = me_ref[0]
    small = stage([(state_ref, state), (pick_ref, pick), (base_ref, base)], in_sem)
    whole = [pltpu.make_async_copy(rows_ref.at[(me >> 1) ^ d], rows.at[d], row_sem.at[d]) for d in range(chips)]
    for copy in whole:
        copy.start()
    for copy in small:
        copy.wait()
    inj_h, inj_t = newton(state[0], state[1], pick[:blocks], pick[blocks:2 * blocks], pick[2 * blocks:],
                          state[2], state[3])
    inj[0] = inj_h
    inj[1] = inj_t
    outs = [pltpu.make_async_copy(inj, inj_ref, in_sem.at[0])]
    outs[0].start()
    order = list(range(chips // 2, chips)) + list(range(chips // 2))
    pending = [None, None]
    for i, d in enumerate(order):
        slot = i % 2
        blk = (me >> 1) ^ d
        scale_h = jnp.broadcast_to(inj[0, pl.ds(blk, 1), :], (LANES, LANES)).T
        scale_t = jnp.broadcast_to(inj[1, pl.ds(blk, 1), :], (LANES, LANES)).T
        whole[d].wait()
        for copy in pending[slot] or ():
            copy.wait()
        for t in range(width):
            at = slice(t * LANES, (t + 1) * LANES)
            value = scale_h * rows[d, 0, t] + scale_t * rows[d, 1, t]
            dev[slot, :, at] = value
            unit[slot, at, :] = ((base[t:t + 1, :] + value) * (1.0 / math.pi)).T
        goal = dev_ref.at[pl.ds(pl.multiple_of(blk * LANES, LANES), LANES)]
        pending[slot] = stage([(dev.at[slot], goal), (unit.at[slot], units[d])], out_sem.at[slot])
    for copy in pending[0] + pending[1] + outs:
        copy.wait()


def prep_kernel(unit, chips, me_ref, from_ref, to_ref, slot_ref, sus_ref, rate_ref,
                f_ref, t_ref, ratio_ref, k_ref, cnt_ref):
    half = f_ref.shape[0]
    me = me_ref[0]
    start = (me & 1) * half
    flip = me * unit
    bits = unit.bit_length() - 1
    slot = columns([slot_ref[...].astype(jnp.float32)])

    square = (LANES, LANES)
    before = lax.broadcasted_iota(jnp.int32, square, 0) < lax.broadcasted_iota(jnp.int32, square, 1)
    before = jnp.where(before, 1.0, 0.0).astype(jnp.bfloat16)
    lane = lax.broadcasted_iota(jnp.int32, (1, LANES), 1).astype(jnp.float32)
    slots = lax.broadcasted_iota(jnp.int32, (GROUP * LANES, LANES), 0).astype(jnp.float32)

    def place(bus_ref, row):
        bus = jnp.concatenate([bus_ref[pl.ds(row + i, 1), :] for i in range(GROUP)], 1)
        rel = lookup(slot, bus)[0].astype(jnp.int32) ^ flip
        chip = rel >> (bits + 1)
        core = (rel >> bits) & 1
        return chip, (rel & (unit - 1)) + (core * chips + chip) * unit

    def group(g, carry):
        f_chip, f = place(from_ref, start + g * GROUP)
        t_chip, t = place(to_ref, start + g * GROUP)
        chip = jnp.maximum(f_chip, t_chip)
        first = jnp.where(chip < chips - 2, 1.0, 0.0)
        second = jnp.where(chip == chips - 2, 1.0, 0.0)
        tile = lambda a, i: a[:, i * LANES:(i + 1) * LANES]
        flags = jnp.concatenate([tile(a, i) for a in (first, second) for i in range(GROUP)], 0)
        ahead = jnp.dot(flags.astype(jnp.bfloat16), before, preferred_element_type=jnp.float32)
        sums = jnp.sum(flags, axis=1, keepdims=True)
        n_first = sum(sums[i:i + 1] for i in range(GROUP))
        n_second = sum(sums[GROUP + i:GROUP + i + 1] for i in range(GROUP))
        off_first = off_second = jnp.zeros((1, 1), jnp.float32)
        total = jnp.zeros((16, GROUP * LANES), jnp.float32)
        for i in range(GROUP):
            c_first = off_first + ahead[i:i + 1]
            c_second = off_second + ahead[GROUP + i:GROUP + i + 1]
            rest = n_first + n_second + (lane + float(i * LANES)) - c_first - c_second
            goal = jnp.where(tile(first, i) > 0.5, c_first,
                             jnp.where(tile(second, i) > 0.5, n_first + c_second, rest))
            off_first = off_first + sums[i:i + 1]
            off_second = off_second + sums[GROUP + i:GROUP + i + 1]
            hot = jnp.where(slots == goal, 1.0, 0.0).astype(jnp.bfloat16)
            row = pl.ds(start + g * GROUP + i, 1)
            rows = [tile(f, i) >> 7, tile(f, i) & 127, tile(t, i) >> 7, tile(t, i) & 127]
            rows = [r.astype(jnp.float32) for r in rows]
            rows += [p.astype(jnp.float32) for p in split(sus_ref[row, :] / rate_ref[row, :], 3)]
            rows += [jnp.full((1, LANES), float(i)), lane] + [jnp.zeros((1, LANES), jnp.float32)] * 7
            values = jnp.concatenate(rows, 0).astype(jnp.bfloat16)
            total += lax.dot_general(values, hot, (((1,), (1,)), ((), ())), preferred_element_type=jnp.float32)
        for i in range(GROUP):
            out = pl.ds(g * GROUP + i, 1)
            part = total[:, i * LANES:(i + 1) * LANES]
            f_ref[out, :] = (part[0:1] * 128.0 + part[1:2]).astype(jnp.int32)
            t_ref[out, :] = (part[2:3] * 128.0 + part[3:4]).astype(jnp.int32)
            ratio_ref[out, :] = part[4:5] + part[5:6] + part[6:7]
            origin = ((start + g * GROUP) * LANES).astype(jnp.float32)
            k_ref[out, :] = part[7:8] * 128.0 + part[8:9] + origin
        wide = lambda a: jnp.broadcast_to(a, (1, LANES)).astype(jnp.int32) >> 7
        cnt_ref[0, pl.ds(g, 1), :] = wide(n_first)
        cnt_ref[1, pl.ds(g, 1), :] = wide(n_first + n_second)
        return carry

    lax.fori_loop(0, half // GROUP, group, 0)


def join_kernel(_, *refs):
    pieces, (out_ref, sem) = refs[:-2], refs[-2:]
    unit = pieces[0].shape[0]
    for copy in stage([(p, out_ref.at[pl.ds(i * unit, unit)]) for i, p in enumerate(pieces)], sem):
        copy.wait()


def worst_kernel(level, me_ref, f_ref, t_ref, cnt_ref, ratio_ref, k_ref, state_ref, *rest):
    n = 2 * level + 2
    if level:
        best_in, *rest = rest
    pieces, (best, table, f_s, t_s, cnt_s, diff, sem) = rest[:n], rest[n:]
    pairs = [(f_ref, f_s), (t_ref, t_s), (cnt_ref, cnt_s)]
    row = 0
    for own, other in zip(pieces[::2], pieces[1::2]):
        size = own.shape[0]
        pairs += [(own, table.at[pl.ds(row, size)]),
                  (other, table.at[pl.ds(table.shape[0] // 2 + row, size)])]
        row += size
    copies = stage(pairs, sem)
    half = f_ref.shape[0]
    ids = state_ref[6, pl.ds(me_ref[0] >> 1, 1), :]
    best[...] = best_in[...] if level else jnp.zeros_like(best)
    for copy in copies:
        copy.wait()

    def block(b, carry):
        for j in range(LANES):
            diff[pl.ds(j, 1), :] = table[pl.ds(f_s[b, j], 1), :] - table[pl.ds(t_s[b, j], 1), :]
        turn = diff[...]
        turn = turn - jnp.round(turn)
        square = turn * turn
        poly = SINE[4]
        for c in SINE[3::-1]:
            poly = poly * square + c
        ratio = jnp.broadcast_to(ratio_ref[pl.ds(b, 1), :], (LANES, LANES)).T
        branch = jnp.broadcast_to(k_ref[pl.ds(b, 1), :], (LANES, LANES)).T
        load = jnp.where(branch == ids, 0.0, jnp.abs(turn * poly) * ratio)
        best[...] = jnp.maximum(best[...], jnp.max(load.reshape(LANES // 8, 8, LANES), axis=0))
        return carry

    def group(g, carry):
        low = cnt_s[level - 1, g, 0] if level else 0
        high = GROUP if level == 2 else cnt_s[level, g, 0]
        return lax.fori_loop(g * GROUP + low, g * GROUP + high, block, carry)

    lax.fori_loop(0, half // GROUP, group, 0)
    if level == 2:
        best[...] = jnp.broadcast_to(jnp.max(best[...], axis=0, keepdims=True), best.shape)


def per_device(
    outages, branch_from, branch_to, bus_slot, susceptance, charging, rating, base_angles, zinv
):
    n_col = lax.axis_size("col")
    buses, cols = zinv.shape
    own = outages.shape[0]
    total = own * n_col
    blocks = total // LANES
    chips = n_col // 2
    assert own * 2 == LANES and chips & (chips - 1) == 0 and chips > 2
    me = lax.axis_index("col")
    where = jnp.stack([me, jnp.int32(n_col)])
    tab = lambda a: a.reshape(-1, LANES)
    from2, to2, slot2, sus2, chg2, rate2, base2 = map(
        tab, (branch_from, branch_to, bus_slot, susceptance, charging, rating, base_angles)
    )
    i32 = lambda *s: jax.ShapeDtypeStruct(s, jnp.int32)
    f32 = lambda *s: jax.ShapeDtypeStruct(s, jnp.float32)

    flat = zinv.reshape(buses // 8, 8, cols // LANES, LANES).transpose(0, 2, 1, 3).reshape(-1, LANES)
    ids = lax.dynamic_update_slice(jnp.zeros((total,), jnp.int32), outages, (me * own,))
    ids = lax.psum(ids[None], "col")

    width = cols // LANES
    like = lambda a: pltpu.VMEM(a.shape, a.dtype)
    row_shape = (2, width, LANES, LANES)
    state, picks, own_base, rows = pl.pallas_call(
        functools.partial(ends_kernel, width),
        name="ends",
        out_shape=[f32(7, blocks, LANES), f32(3 * blocks, LANES), f32(width, LANES), f32(blocks, *row_shape)],
        in_specs=[SMEM, VMEM] + [ANY] * 7,
        out_specs=[VMEM] * 3 + [ANY],
        scratch_shapes=[like(from2), like(to2), like(slot2), like(sus2), like(chg2), like(base2), like(flat),
                        pltpu.VMEM((2 * blocks, LANES), jnp.int32), pltpu.SMEM((2 * blocks, LANES), jnp.int32),
                        pltpu.VMEM((2,) + row_shape, jnp.float32), pltpu.SemaphoreType.DMA((7,)),
                        pltpu.SemaphoreType.DMA((2,))],
        compiler_params=params(60),
    )(where, ids, from2, to2, slot2, sus2, chg2, base2, flat)

    swap = lambda a, m: lax.ppermute(a, "col", [(i, i ^ m) for i in range(n_col)])
    step = 1
    while step < n_col:
        picks = sum([swap(picks, m * step) for m in range(1, min(4, n_col // step))], picks)
        step *= 4

    injections, deviation, *units = pl.pallas_call(
        functools.partial(spread_kernel, chips),
        name="spread",
        out_shape=[f32(2, blocks, LANES), f32(total, cols)] + [f32(cols, LANES)] * chips,
        in_specs=[SMEM] + [ANY] * 4,
        out_specs=[ANY] * (2 + chips),
        scratch_shapes=[like(state), like(picks), like(own_base), pltpu.VMEM((2, blocks, LANES), jnp.float32),
                        like(rows), pltpu.VMEM((2, LANES, cols), jnp.float32),
                        pltpu.VMEM((2, cols, LANES), jnp.float32), pltpu.SemaphoreType.DMA((3,)),
                        pltpu.SemaphoreType.DMA((chips,)), pltpu.SemaphoreType.DMA((2, 2))],
        compiler_params=params(60),
    )(where, state, picks, own_base, rows)

    half = branch_from.shape[0] // LANES // 2
    f_rel, t_rel, ratio, k_rel, counts = pl.pallas_call(
        functools.partial(prep_kernel, cols, chips),
        name="prep",
        out_shape=[i32(half, LANES), i32(half, LANES), f32(half, LANES), f32(half, LANES),
                   i32(2, half // GROUP, LANES)],
        in_specs=[SMEM] + [VMEM] * 5,
        out_specs=[VMEM] * 5,
        compiler_params=params(16),
    )(where, from2, to2, slot2, sus2, rate2)

    got = [units[0]] + [swap(units[d], 2 * d) for d in range(1, chips)]

    def join(after, pieces):
        packed = pl.pallas_call(
            join_kernel,
            name="join",
            out_shape=f32(len(pieces) * cols, LANES),
            in_specs=[ANY] * (1 + len(pieces)),
            out_specs=VMEM,
            scratch_shapes=[pltpu.SemaphoreType.DMA((len(pieces),))],
            compiler_params=params(16),
        )(after, *pieces)
        return [packed, swap(packed, 1)]

    def worst_of(level, *operands):
        return pl.pallas_call(
            functools.partial(worst_kernel, level),
            name=f"worst{level}",
            out_shape=f32(8, LANES),
            in_specs=[SMEM] + [ANY] * 3 + [VMEM] * (3 + min(level, 1)) + [ANY] * (2 * level + 2),
            out_specs=VMEM,
            scratch_shapes=[pltpu.VMEM((buses, LANES), jnp.float32)]
            + [pltpu.SMEM(a.shape, a.dtype) for a in (f_rel, t_rel, counts)]
            + [pltpu.VMEM((LANES, LANES), jnp.float32), pltpu.SemaphoreType.DMA((2 * level + 5,))],
            compiler_params=params(16),
        )(where, f_rel, t_rel, counts, ratio, k_rel, state, *operands)

    early = join(counts, got[:-2])
    best = worst_of(0, *early)
    middle, late = join(best, got[-2:-1]), join(best, got[-1:])
    best = worst_of(1, best, *early, *middle)
    best = worst_of(2, best, *early, *middle, *late)
    worst = lax.slice(best, (0, 0), (1, LANES))
    worst = lax.dynamic_slice(jnp.maximum(worst, swap(worst, 1))[0], ((me & 1) * own,), (own,))
    inj = lax.dynamic_slice(injections.reshape(2, total), (0, me * own), (2, own))
    return inj, deviation, worst


def solution(mesh):
    return jax.shard_map(
        per_device,
        mesh=mesh,
        in_specs=(P(("parts", "col")), P(), P(), P(), P(), P(), P(), P("parts"), P(None, "col")),
        out_specs=(P(None, ("parts", "col")), P("parts", "col"), P(("parts", "col"))),
        check_vma=False,
    )
```

```python
import functools
import math

import jax
import jax.numpy as jnp
from jax import lax
from jax.experimental import pallas as pl
from jax.experimental.pallas import tpu as pltpu
from jax.sharding import PartitionSpec as P

STEPS = 3
LANES = 128
LATE = 2
CHUNKS = 1
GROUP = 4
SINE = (3.1415926444, -5.1677100819, 2.5500775297, -0.5982913039, 0.0776576582)
VMEM = pl.BlockSpec(memory_space=pltpu.VMEM)
SMEM = pl.BlockSpec(memory_space=pltpu.SMEM)
ANY = pl.BlockSpec(memory_space=pl.ANY)


def params(mib):
    return pltpu.CompilerParams(vmem_limit_bytes=mib * 2**20)


def split(table, parts):
    out = []
    for _ in range(parts):
        piece = table.astype(jnp.bfloat16)
        out.append(piece)
        table = table - piece.astype(jnp.float32)
    return out


def columns(tables):
    return jnp.concatenate([jnp.concatenate(split(t.T, 3), 1) for t in tables], 0)


def lookup(turned, index):
    rows = turned.shape[1] // 3
    n = index.shape[1]
    hot = lax.broadcasted_iota(jnp.int32, (rows, n), 0) == (index >> 7)
    hot = jnp.where(hot, 1.0, 0.0).astype(jnp.bfloat16)
    picked = jnp.dot(turned, jnp.concatenate([hot] * 3, 0), preferred_element_type=jnp.float32)
    lane = lax.broadcasted_iota(jnp.int32, (LANES, n), 0) == (index & 127)
    return [jnp.sum(jnp.where(lane, picked[i:i + LANES], 0.0), axis=0, keepdims=True)
            for i in range(0, turned.shape[0], LANES)]


def newton(a_head, a_tail, self_head, cross, self_tail, bsus, hchg):
    inj_head = jnp.zeros_like(a_head)
    inj_tail = jnp.zeros_like(a_head)
    for step in range(1, STEPS + 1):
        level = step / STEPS
        end_head = a_head + self_head * inj_head + cross * inj_tail
        end_tail = a_tail + cross * inj_head + self_tail * inj_tail
        spread = end_head - end_tail
        sine_val = jnp.sin(spread)
        cosine_val = jnp.cos(spread)
        resid_head = inj_head - level * (bsus * sine_val + hchg * end_head)
        resid_tail = inj_tail - level * (-bsus * sine_val + hchg * end_tail)
        diag_term = bsus * cosine_val + hchg
        cross_term = -bsus * cosine_val
        jac_one = 1.0 - level * (diag_term * self_head + cross_term * cross)
        jac_two = -level * (diag_term * cross + cross_term * self_tail)
        jac_three = -level * (cross_term * self_head + diag_term * cross)
        jac_four = 1.0 - level * (cross_term * cross + diag_term * self_tail)
        determinant = jac_one * jac_four - jac_two * jac_three
        inj_head = inj_head - (jac_four * resid_head - jac_two * resid_tail) / determinant
        inj_tail = inj_tail - (jac_one * resid_tail - jac_three * resid_head) / determinant
    return inj_head, inj_tail


def addresses(row, width):
    return (row >> 3) * (8 * width) + (row & 7)


def stage(pairs, sem):
    copies = [pltpu.make_async_copy(src, dst, sem.at[i]) for i, (src, dst) in enumerate(pairs)]
    for copy in copies:
        copy.start()
    return copies


def ends_kernel(width, me_ref, ids_ref, from_ref, to_ref, slot_ref, sus_ref, chg_ref, base_ref, zinv_ref,
                state_ref, pick_ref, own_base_ref, rows_ref, from_v, to_v, slot_v, sus_v, chg_v, base_v,
                zinv_v, ends_v, ends_s, rows, sem, out_sem, zinv_sem):
    total = ids_ref.shape[1]
    blocks = total // LANES
    first = me_ref[0] * width * LANES
    copies = stage([(from_ref, from_v), (to_ref, to_v), (slot_ref, slot_v), (sus_ref, sus_v),
                    (chg_ref, chg_v), (base_ref, base_v)], sem)
    part = zinv_v.shape[0] // CHUNKS
    cuts = [pl.ds(i * part, part) for i in range(CHUNKS)]
    zinv_copies = stage([(zinv_ref.at[c], zinv_v.at[c]) for c in cuts], zinv_sem)
    for copy in copies:
        copy.wait()
    branch = columns([from_v[...].astype(jnp.float32), to_v[...].astype(jnp.float32), sus_v[...], chg_v[...]])
    slot = columns([slot_v[...].astype(jnp.float32)])
    base = columns([base_v[...]])
    wide = min(total, 8 * LANES)
    for c in range(0, total, wide):
        ids = ids_ref[:, c:c + wide]
        f, t, sus, chg = lookup(branch, ids)
        ends, = lookup(slot, jnp.concatenate([f, t], 1).astype(jnp.int32))
        ends = ends.astype(jnp.int32)
        angle, = lookup(base, ends)
        place = addresses(ends, width)
        local = (ends - first).astype(jnp.float32)
        known = (angle[:, :wide], angle[:, wide:], sus, chg, local[:, :wide], local[:, wide:],
                 ids.astype(jnp.float32))
        for b in range(wide // LANES):
            row = slice(c // LANES + b, c // LANES + b + 1)
            at = slice(b * LANES, (b + 1) * LANES)
            ends_v[row, :] = place[:, at]
            ends_v[slice(blocks + row.start, blocks + row.stop), :] = place[:, b * LANES + wide:(b + 1) * LANES + wide]
            for i, value in enumerate(known):
                state_ref[i, row, :] = value[:, at]
    copy = pltpu.make_async_copy(ends_v, ends_s, sem.at[0])
    copy.start()
    for t in range(width):
        own_base_ref[t:t + 1, :] = base_v[pl.ds(me_ref[0] * width + t, 1), :]
    copy.wait()
    for copy in zinv_copies:
        copy.wait()

    def block(b, slot):
        def fetch(g, carry):
            for i in range(32):
                o = g * 32 + i
                head = ends_s[b, o]
                tail = ends_s[blocks + b, o]
                for t in range(width):
                    rows[slot, 0, t, pl.ds(o, 1), :] = zinv_v[pl.ds(head + 8 * t, 1), :]
                    rows[slot, 1, t, pl.ds(o, 1), :] = zinv_v[pl.ds(tail + 8 * t, 1), :]
            return carry

        lax.fori_loop(0, LANES // 32, fetch, 0)
        pltpu.make_async_copy(rows.at[slot], rows_ref.at[b], out_sem.at[slot]).start()
        square = (LANES, LANES)
        at_h = jnp.broadcast_to(state_ref[4, pl.ds(b, 1), :], square).T
        at_t = jnp.broadcast_to(state_ref[5, pl.ds(b, 1), :], square).T
        lane = lax.broadcasted_iota(jnp.int32, square, 1).astype(jnp.float32)
        hh = ht = tt = jnp.zeros(square, jnp.float32)
        for t in range(width):
            is_h = at_h == lane + float(t * LANES)
            is_t = at_t == lane + float(t * LANES)
            hh = jnp.where(is_h, rows[slot, 0, t], hh)
            ht = jnp.where(is_t, rows[slot, 0, t], ht)
            tt = jnp.where(is_t, rows[slot, 1, t], tt)
        for i, pick in enumerate((hh, ht, tt)):
            pick_ref[pl.ds(i * blocks + b, 1), :] = jnp.sum(pick.T, axis=0, keepdims=True)

    def pair(i, carry):
        for slot in (0, 1):
            @pl.when(i > 0)
            def _():
                pltpu.make_async_copy(rows.at[slot], rows_ref.at[2 * i - 2 + slot], out_sem.at[slot]).wait()

            block(2 * i + slot, slot)
        return carry

    lax.fori_loop(0, blocks // 2, pair, 0)
    for slot in (0, 1):
        pltpu.make_async_copy(rows.at[slot], rows_ref.at[blocks - 2 + slot], out_sem.at[slot]).wait()


def spread_kernel(chips, me_ref, state_ref, pick_ref, base_ref, rows_ref, inj_ref, dev_ref, *rest):
    units, (state, pick, base, inj, rows, dev, unit, in_sem, row_sem, out_sem) = rest[:chips], rest[chips:]
    blocks, _, width = rows.shape[:3]
    me = me_ref[0]
    small = stage([(state_ref, state), (pick_ref, pick), (base_ref, base)], in_sem)
    whole = [pltpu.make_async_copy(rows_ref.at[(me >> 1) ^ d], rows.at[d], row_sem.at[d]) for d in range(chips)]
    for copy in whole:
        copy.start()
    for copy in small:
        copy.wait()
    inj_h, inj_t = newton(state[0], state[1], pick[:blocks], pick[blocks:2 * blocks], pick[2 * blocks:],
                          state[2], state[3])
    inj[0] = inj_h
    inj[1] = inj_t
    outs = [pltpu.make_async_copy(inj, inj_ref, in_sem.at[0])]
    outs[0].start()
    order = list(range(chips // 2, chips)) + list(range(chips // 2))
    pending = [None, None]
    for i, d in enumerate(order):
        slot = i % 2
        blk = (me >> 1) ^ d
        scale_h = jnp.broadcast_to(inj[0, pl.ds(blk, 1), :], (LANES, LANES)).T
        scale_t = jnp.broadcast_to(inj[1, pl.ds(blk, 1), :], (LANES, LANES)).T
        whole[d].wait()
        for copy in pending[slot] or ():
            copy.wait()
        for t in range(width):
            at = slice(t * LANES, (t + 1) * LANES)
            value = scale_h * rows[d, 0, t] + scale_t * rows[d, 1, t]
            dev[slot, :, at] = value
            unit[slot, at, :] = ((base[t:t + 1, :] + value) * (1.0 / math.pi)).T
        goal = dev_ref.at[pl.ds(pl.multiple_of(blk * LANES, LANES), LANES)]
        pending[slot] = stage([(dev.at[slot], goal), (unit.at[slot], units[d])], out_sem.at[slot])
    for copy in pending[0] + pending[1] + outs:
        copy.wait()


def prep_kernel(unit, chips, me_ref, from_ref, to_ref, slot_ref, sus_ref, rate_ref,
                f_ref, t_ref, ratio_ref, k_ref, cnt_ref):
    half = ratio_ref.shape[0]
    groups = half // GROUP
    me = me_ref[0]
    start = (me & 1) * half
    flip = me * unit
    bits = unit.bit_length() - 1
    slot = columns([slot_ref[...].astype(jnp.float32)])

    square = (LANES, LANES)
    before = lax.broadcasted_iota(jnp.int32, square, 0) < lax.broadcasted_iota(jnp.int32, square, 1)
    before = jnp.where(before, 1.0, 0.0).astype(jnp.bfloat16)
    lane = lax.broadcasted_iota(jnp.int32, (1, LANES), 1).astype(jnp.float32)
    slots = lax.broadcasted_iota(jnp.int32, (GROUP * LANES, LANES), 0).astype(jnp.float32)
    cnt_ref[...] = jnp.zeros_like(cnt_ref)

    def place(bus_ref, row):
        bus = jnp.concatenate([bus_ref[pl.ds(row + i, 1), :] for i in range(GROUP)], 1)
        rel = lookup(slot, bus)[0].astype(jnp.int32) ^ flip
        chip = rel >> (bits + 1)
        core = (rel >> bits) & 1
        return chip, (rel & (unit - 1)) + (core * chips + chip) * unit

    def group(g, carry):
        f_chip, f = place(from_ref, start + g * GROUP)
        t_chip, t = place(to_ref, start + g * GROUP)
        first = jnp.where(jnp.maximum(f_chip, t_chip) < chips - LATE, 1.0, 0.0)
        tile = lambda a, i: a[:, i * LANES:(i + 1) * LANES]
        flags = jnp.concatenate([tile(first, i) for i in range(GROUP)]
                                + [jnp.zeros((8 - GROUP, LANES), jnp.float32)], 0)
        ahead = jnp.dot(flags.astype(jnp.bfloat16), before, preferred_element_type=jnp.float32)
        sums = jnp.sum(flags, axis=1, keepdims=True)
        count = sum(sums[i:i + 1] for i in range(GROUP))
        offset = jnp.zeros((1, 1), jnp.float32)
        total = jnp.zeros((16, GROUP * LANES), jnp.float32)
        for i in range(GROUP):
            front = offset + ahead[i:i + 1]
            rest = count + (lane + float(i * LANES)) - front
            goal = jnp.where(tile(first, i) > 0.5, front, rest)
            offset = offset + sums[i:i + 1]
            hot = jnp.where(slots == goal, 1.0, 0.0).astype(jnp.bfloat16)
            row = pl.ds(start + g * GROUP + i, 1)
            rows = [tile(f, i) >> 7, tile(f, i) & 127, tile(t, i) >> 7, tile(t, i) & 127]
            rows = [r.astype(jnp.float32) for r in rows]
            rows += [p.astype(jnp.float32) for p in split(sus_ref[row, :] / rate_ref[row, :], 3)]
            rows += [jnp.full((1, LANES), float(i)), lane] + [jnp.zeros((1, LANES), jnp.float32)] * 7
            values = jnp.concatenate(rows, 0).astype(jnp.bfloat16)
            total += lax.dot_general(values, hot, (((1,), (1,)), ((), ())), preferred_element_type=jnp.float32)
        for i in range(GROUP):
            out = pl.ds(i * groups + g, 1)
            part = total[:, i * LANES:(i + 1) * LANES]
            f_ref[out, :] = (part[0:1] * 128.0 + part[1:2]).astype(jnp.int32)
            t_ref[out, :] = (part[2:3] * 128.0 + part[3:4]).astype(jnp.int32)
            ratio_ref[out, :] = part[4:5] + part[5:6] + part[6:7]
            origin = ((start + g * GROUP) * LANES).astype(jnp.float32)
            k_ref[out, :] = part[7:8] * 128.0 + part[8:9] + origin
        blocks = jnp.broadcast_to(count, (1, LANES)).astype(jnp.int32) >> 7
        cnt_ref[...] = jnp.where(lane == g.astype(jnp.float32), blocks, cnt_ref[...])
        return carry

    lax.fori_loop(0, half // GROUP, group, 0)


def join_kernel(_, *refs):
    pieces, (out_ref, sem) = refs[:-2], refs[-2:]
    unit = pieces[0].shape[0]
    for copy in stage([(p, out_ref.at[pl.ds(i * unit, unit)]) for i, p in enumerate(pieces)], sem):
        copy.wait()


def worst_kernel(late, me_ref, f_ref, t_ref, cnt_ref, ratio_ref, k_ref, state_ref, *rest):
    if late:
        best_ref, *rest = rest
    pieces, (out_ref, table, f_s, t_s, cnt_s, best, diff, sem) = rest[:2 * late + 2], rest[2 * late + 2:]
    half = f_ref.shape[0]
    groups = half // GROUP
    side = [pl.ds(0, half // 2), pl.ds(half // 2, half // 2)]
    main, spare = side[late], side[1 - late]
    pairs = [(cnt_ref, cnt_s), (f_ref.at[main], f_s.at[main]), (t_ref.at[main], t_s.at[main])]
    row = 0
    for own, other in zip(pieces[::2], pieces[1::2]):
        size = own.shape[0]
        pairs += [(own, table.at[pl.ds(row, size)]),
                  (other, table.at[pl.ds(table.shape[0] // 2 + row, size)])]
        row += size
    copies = stage(pairs, sem)
    ids = state_ref[6, pl.ds(me_ref[0] >> 1, 1), :]
    best[...] = best_ref[...] if late else jnp.zeros_like(best)
    for copy in copies:
        copy.wait()
    bound = cnt_s[0, 0]
    for g in range(1, groups):
        bound = jnp.minimum(bound, cnt_s[0, g]) if late else jnp.maximum(bound, cnt_s[0, g])

    @pl.when(bound < GROUP // 2 if late else bound > GROUP // 2)
    def _():
        for copy in stage([(f_ref.at[spare], f_s.at[spare]), (t_ref.at[spare], t_s.at[spare])], sem):
            copy.wait()

    def group(g, carry):
        def block(i, carry):
            b = i * groups + g
            for j in range(LANES):
                diff[pl.ds(j, 1), :] = table[pl.ds(f_s[b, j], 1), :] - table[pl.ds(t_s[b, j], 1), :]
            turn = diff[...]
            turn = turn - jnp.round(turn)
            square = turn * turn
            poly = SINE[4]
            for c in SINE[3::-1]:
                poly = poly * square + c
            scale = jnp.broadcast_to(ratio_ref[pl.ds(b, 1), :], (LANES, LANES)).T
            branch = jnp.broadcast_to(k_ref[pl.ds(b, 1), :], (LANES, LANES)).T
            load = jnp.where(branch == ids, 0.0, jnp.abs(turn * poly) * scale)
            best[...] = jnp.maximum(best[...], jnp.max(load.reshape(LANES // 8, 8, LANES), axis=0))
            return carry

        return lax.fori_loop(cnt_s[0, g] if late else 0, GROUP if late else cnt_s[0, g], block, carry)

    lax.fori_loop(0, groups, group, 0)
    out_ref[...] = jnp.max(best[...], axis=0, keepdims=True) if late else best[...]


def per_device(
    outages, branch_from, branch_to, bus_slot, susceptance, charging, rating, base_angles, zinv
):
    n_col = lax.axis_size("col")
    buses, cols = zinv.shape
    own = outages.shape[0]
    total = own * n_col
    blocks = total // LANES
    chips = n_col // 2
    assert own * 2 == LANES and chips & (chips - 1) == 0 and chips > 2
    me = lax.axis_index("col")
    where = me[None]
    tab = lambda a: a.reshape(-1, LANES)
    from2, to2, slot2, sus2, chg2, rate2, base2 = map(
        tab, (branch_from, branch_to, bus_slot, susceptance, charging, rating, base_angles)
    )
    i32 = lambda *s: jax.ShapeDtypeStruct(s, jnp.int32)
    f32 = lambda *s: jax.ShapeDtypeStruct(s, jnp.float32)

    flat = zinv.reshape(buses // 8, 8, cols // LANES, LANES).transpose(0, 2, 1, 3).reshape(-1, LANES)
    ids = lax.dynamic_update_slice(jnp.zeros((total,), jnp.int32), outages, (me * own,))
    ids = lax.psum(ids[None], "col")

    width = cols // LANES
    like = lambda a: pltpu.VMEM(a.shape, a.dtype)
    row_shape = (2, width, LANES, LANES)
    state, picks, own_base, rows = pl.pallas_call(
        functools.partial(ends_kernel, width),
        name="ends",
        out_shape=[f32(7, blocks, LANES), f32(3 * blocks, LANES), f32(width, LANES), f32(blocks, *row_shape)],
        in_specs=[SMEM, VMEM] + [ANY] * 7,
        out_specs=[VMEM] * 3 + [ANY],
        scratch_shapes=[like(from2), like(to2), like(slot2), like(sus2), like(chg2), like(base2), like(flat),
                        pltpu.VMEM((2 * blocks, LANES), jnp.int32), pltpu.SMEM((2 * blocks, LANES), jnp.int32),
                        pltpu.VMEM((2,) + row_shape, jnp.float32), pltpu.SemaphoreType.DMA((6,)),
                        pltpu.SemaphoreType.DMA((2,)), pltpu.SemaphoreType.DMA((CHUNKS,))],
        compiler_params=params(60),
    )(where, ids, from2, to2, slot2, sus2, chg2, base2, flat)

    swap = lambda a, m: lax.ppermute(a, "col", [(i, i ^ m) for i in range(n_col)])
    step = 1
    while step < n_col:
        picks = sum([swap(picks, m * step) for m in range(1, min(4, n_col // step))], picks)
        step *= 4

    injections, deviation, *units = pl.pallas_call(
        functools.partial(spread_kernel, chips),
        name="spread",
        out_shape=[f32(2, blocks, LANES), f32(total, cols)] + [f32(cols, LANES)] * chips,
        in_specs=[SMEM] + [ANY] * 4,
        out_specs=[ANY] * (2 + chips),
        scratch_shapes=[like(state), like(picks), like(own_base), pltpu.VMEM((2, blocks, LANES), jnp.float32),
                        like(rows), pltpu.VMEM((2, LANES, cols), jnp.float32),
                        pltpu.VMEM((2, cols, LANES), jnp.float32), pltpu.SemaphoreType.DMA((3,)),
                        pltpu.SemaphoreType.DMA((chips,)), pltpu.SemaphoreType.DMA((2, 2))],
        compiler_params=params(60),
    )(where, state, picks, own_base, rows)

    half = branch_from.shape[0] // LANES // 2
    f_rel, t_rel, ratio, k_rel, counts = pl.pallas_call(
        functools.partial(prep_kernel, cols, chips),
        name="prep",
        out_shape=[i32(half, LANES), i32(half, LANES), f32(half, LANES), f32(half, LANES),
                   i32(1, LANES)],
        in_specs=[SMEM] + [VMEM] * 5,
        out_specs=[VMEM] * 5,
        compiler_params=params(16),
    )(where, from2, to2, slot2, sus2, rate2)

    got = [units[0]] + [swap(units[d], 2 * d) for d in range(1, chips)]

    def join(after, pieces):
        packed = pl.pallas_call(
            join_kernel,
            name="join",
            out_shape=f32(len(pieces) * cols, LANES),
            in_specs=[ANY] * (1 + len(pieces)),
            out_specs=VMEM,
            scratch_shapes=[pltpu.SemaphoreType.DMA((len(pieces),))],
            compiler_params=params(16),
        )(after, *pieces)
        return [packed, swap(packed, 1)]

    def worst_of(level, *operands):
        return pl.pallas_call(
            functools.partial(worst_kernel, level),
            name=f"worst{level}",
            out_shape=f32(1 if level else 8, LANES),
            in_specs=[SMEM] + [ANY] * 3 + [VMEM] * (3 + level) + [ANY] * (len(operands) - level),
            out_specs=VMEM,
            scratch_shapes=[pltpu.VMEM((buses, LANES), jnp.float32), pltpu.SMEM(f_rel.shape, jnp.int32),
                            pltpu.SMEM(t_rel.shape, jnp.int32), pltpu.SMEM(counts.shape, jnp.int32),
                            pltpu.VMEM((8, LANES), jnp.float32), pltpu.VMEM((LANES, LANES), jnp.float32),
                            pltpu.SemaphoreType.DMA((3 + len(operands),))],
            compiler_params=params(16),
        )(where, f_rel, t_rel, counts, ratio, k_rel, state, *operands)

    early = join(counts, got[:-LATE])
    best = worst_of(0, *early)
    worst = worst_of(1, best, *early, *join(best, got[-LATE:]))
    mine = lambda a, b: lax.dynamic_slice(a, (jnp.int32(0),) * (a.ndim - len(b)) + b, a.shape[:1] + (1,) * (a.ndim - 2) + (own,))
    worst = jnp.maximum(mine(worst, ((me & 1) * own,)), mine(swap(worst, 1), ((me & 1) * own,))).reshape(own)
    inj = mine(injections, (me >> 1, (me & 1) * own)).reshape(2, own)
    return inj, deviation, worst


def solution(mesh):
    return jax.shard_map(
        per_device,
        mesh=mesh,
        in_specs=(P(("parts", "col")), P(), P(), P(), P(), P(), P(), P("parts"), P(None, "col")),
        out_specs=(P(None, ("parts", "col")), P("parts", "col"), P(("parts", "col"))),
        check_vma=False,
    )
```

```python
import functools
import math

import jax
import jax.numpy as jnp
from jax import lax
from jax.experimental import pallas as pl
from jax.experimental.pallas import tpu as pltpu
from jax.sharding import PartitionSpec as P

STEPS = 3
LANES = 128
LATE = 2
CHUNKS = 1
GROUP = 4
SINE = (3.1415926444, -5.1677100819, 2.5500775297, -0.5982913039, 0.0776576582)
VMEM = pl.BlockSpec(memory_space=pltpu.VMEM)
SMEM = pl.BlockSpec(memory_space=pltpu.SMEM)
ANY = pl.BlockSpec(memory_space=pl.ANY)


def params(mib):
    return pltpu.CompilerParams(vmem_limit_bytes=mib * 2**20)


def split(table, parts):
    out = []
    for _ in range(parts):
        piece = table.astype(jnp.bfloat16)
        out.append(piece)
        table = table - piece.astype(jnp.float32)
    return out


def columns(tables):
    return jnp.concatenate([jnp.concatenate(split(t.T, 3), 1) for t in tables], 0)


def lookup(turned, index):
    rows = turned.shape[1] // 3
    n = index.shape[1]
    hot = lax.broadcasted_iota(jnp.int32, (rows, n), 0) == (index >> 7)
    hot = jnp.where(hot, 1.0, 0.0).astype(jnp.bfloat16)
    picked = jnp.dot(turned, jnp.concatenate([hot] * 3, 0), preferred_element_type=jnp.float32)
    lane = lax.broadcasted_iota(jnp.int32, (LANES, n), 0) == (index & 127)
    return [jnp.sum(jnp.where(lane, picked[i:i + LANES], 0.0), axis=0, keepdims=True)
            for i in range(0, turned.shape[0], LANES)]


def newton(a_head, a_tail, self_head, cross, self_tail, bsus, hchg):
    inj_head = jnp.zeros_like(a_head)
    inj_tail = jnp.zeros_like(a_head)
    for step in range(1, STEPS + 1):
        level = step / STEPS
        end_head = a_head + self_head * inj_head + cross * inj_tail
        end_tail = a_tail + cross * inj_head + self_tail * inj_tail
        spread = end_head - end_tail
        sine_val = jnp.sin(spread)
        cosine_val = jnp.cos(spread)
        resid_head = inj_head - level * (bsus * sine_val + hchg * end_head)
        resid_tail = inj_tail - level * (-bsus * sine_val + hchg * end_tail)
        diag_term = bsus * cosine_val + hchg
        cross_term = -bsus * cosine_val
        jac_one = 1.0 - level * (diag_term * self_head + cross_term * cross)
        jac_two = -level * (diag_term * cross + cross_term * self_tail)
        jac_three = -level * (cross_term * self_head + diag_term * cross)
        jac_four = 1.0 - level * (cross_term * cross + diag_term * self_tail)
        determinant = jac_one * jac_four - jac_two * jac_three
        inj_head = inj_head - (jac_four * resid_head - jac_two * resid_tail) / determinant
        inj_tail = inj_tail - (jac_one * resid_tail - jac_three * resid_head) / determinant
    return inj_head, inj_tail


def addresses(row, width):
    return (row >> 3) * (8 * width) + (row & 7)


def stage(pairs, sem):
    copies = [pltpu.make_async_copy(src, dst, sem.at[i]) for i, (src, dst) in enumerate(pairs)]
    for copy in copies:
        copy.start()
    return copies


def ends_kernel(width, me_ref, ids_ref, from_ref, to_ref, slot_ref, sus_ref, chg_ref, base_ref, zinv_ref,
                state_ref, pick_ref, rows_ref, from_v, to_v, slot_v, sus_v, chg_v, base_v,
                zinv_v, ends_v, ends_s, rows, sem, out_sem, zinv_sem):
    total = ids_ref.shape[1]
    blocks = total // LANES
    first = me_ref[0] * width * LANES
    copies = stage([(from_ref, from_v), (to_ref, to_v), (slot_ref, slot_v), (sus_ref, sus_v),
                    (chg_ref, chg_v), (base_ref, base_v)], sem)
    part = zinv_v.shape[0] // CHUNKS
    cuts = [pl.ds(i * part, part) for i in range(CHUNKS)]
    zinv_copies = stage([(zinv_ref.at[c], zinv_v.at[c]) for c in cuts], zinv_sem)
    for copy in copies:
        copy.wait()
    branch = columns([from_v[...].astype(jnp.float32), to_v[...].astype(jnp.float32), sus_v[...], chg_v[...]])
    slot = columns([slot_v[...].astype(jnp.float32)])
    base = columns([base_v[...]])
    wide = min(total, 8 * LANES)
    for c in range(0, total, wide):
        ids = ids_ref[:, c:c + wide]
        f, t, sus, chg = lookup(branch, ids)
        ends, = lookup(slot, jnp.concatenate([f, t], 1).astype(jnp.int32))
        ends = ends.astype(jnp.int32)
        angle, = lookup(base, ends)
        place = addresses(ends, width)
        local = (ends - first).astype(jnp.float32)
        known = (angle[:, :wide], angle[:, wide:], sus, chg, local[:, :wide], local[:, wide:],
                 ids.astype(jnp.float32))
        for b in range(wide // LANES):
            row = slice(c // LANES + b, c // LANES + b + 1)
            at = slice(b * LANES, (b + 1) * LANES)
            ends_v[row, :] = place[:, at]
            ends_v[slice(blocks + row.start, blocks + row.stop), :] = place[:, b * LANES + wide:(b + 1) * LANES + wide]
            for i, value in enumerate(known):
                state_ref[i, row, :] = value[:, at]
    copy = pltpu.make_async_copy(ends_v, ends_s, sem.at[0])
    copy.start()
    for t in range(width):
        state_ref[7, t:t + 1, :] = base_v[pl.ds(me_ref[0] * width + t, 1), :]
    copy.wait()
    for copy in zinv_copies:
        copy.wait()

    def fetch(b, slot):
        for o in range(LANES):
            at = pl.ds(o * width, width)
            rows[slot, 0, at, :] = zinv_v[pl.ds(ends_s[b, o], width, stride=8), :]
            rows[slot, 1, at, :] = zinv_v[pl.ds(ends_s[blocks + b, o], width, stride=8), :]

    def choose(b, slot):
        square = (LANES, LANES)
        at_h = jnp.broadcast_to(state_ref[4, pl.ds(b, 1), :], square).T
        at_t = jnp.broadcast_to(state_ref[5, pl.ds(b, 1), :], square).T
        lane = lax.broadcasted_iota(jnp.int32, square, 1).astype(jnp.float32)
        hh = ht = tt = jnp.zeros(square, jnp.float32)
        for t in range(width):
            is_h = at_h == lane + float(t * LANES)
            is_t = at_t == lane + float(t * LANES)
            piece = pl.ds(t, LANES, stride=width)
            row_h, row_t = rows[slot, 0, piece, :], rows[slot, 1, piece, :]
            hh = jnp.where(is_h, row_h, hh)
            ht = jnp.where(is_t, row_h, ht)
            tt = jnp.where(is_t, row_t, tt)
        for i, pick in enumerate((hh, ht, tt)):
            pick_ref[pl.ds(i * blocks + b, 1), :] = jnp.sum(pick.T, axis=0, keepdims=True)

    def send(b, slot):
        return pltpu.make_async_copy(rows.at[slot], rows_ref.at[b], out_sem.at[slot])

    def pair(i, carry):
        for slot in (0, 1):
            b = 2 * i + slot

            @pl.when(i > 0)
            def _():
                send(b - 2, slot).wait()

            fetch(b, slot)
            choose(jnp.maximum(b - 1, 0), 1 - slot)
            send(b, slot).start()
        return carry

    rows[1] = jnp.zeros_like(rows[1])
    lax.fori_loop(0, blocks // 2, pair, 0)
    choose(blocks - 1, 1)
    for slot in (0, 1):
        send(blocks - 2 + slot, slot).wait()


def spread_kernel(chips, terms, me_ref, state_ref, rows_ref, *rest):
    pick_refs, (inj_ref, dev_ref, *rest) = rest[:terms], rest[terms:]
    units, (state, pick, inj, rows, dev, unit, in_sem, row_sem, out_sem) = rest[:chips], rest[chips:]
    blocks, width = chips, dev.shape[2] // LANES
    me = me_ref[0]
    small = stage([(state_ref, state)] + [(p, pick.at[i]) for i, p in enumerate(pick_refs)], in_sem)
    whole = [pltpu.make_async_copy(rows_ref.at[(me >> 1) ^ d], rows.at[d], row_sem.at[d]) for d in range(chips)]
    for copy in whole:
        copy.start()
    for copy in small:
        copy.wait()
    picks = sum(pick[i] for i in range(terms))
    inj_h, inj_t = newton(state[0], state[1], picks[:blocks], picks[blocks:2 * blocks], picks[2 * blocks:],
                          state[2], state[3])
    inj[0] = inj_h
    inj[1] = inj_t
    outs = [pltpu.make_async_copy(inj, inj_ref, in_sem.at[0])]
    outs[0].start()
    order = list(range(chips // 2, chips)) + list(range(chips // 2))
    pending = [None, None]
    for i, d in enumerate(order):
        slot = i % 2
        blk = (me >> 1) ^ d
        scale_h = jnp.broadcast_to(inj[0, pl.ds(blk, 1), :], (LANES, LANES)).T
        scale_t = jnp.broadcast_to(inj[1, pl.ds(blk, 1), :], (LANES, LANES)).T
        whole[d].wait()
        for copy in pending[slot] or ():
            copy.wait()
        for t in range(width):
            at = slice(t * LANES, (t + 1) * LANES)
            piece = pl.ds(t, LANES, stride=width)
            value = scale_h * rows[d, 0, piece, :] + scale_t * rows[d, 1, piece, :]
            dev[slot, :, at] = value
            unit[slot, at, :] = ((state[7, t:t + 1, :] + value) * (1.0 / math.pi)).T
        goal = dev_ref.at[pl.ds(pl.multiple_of(blk * LANES, LANES), LANES)]
        pending[slot] = stage([(dev.at[slot], goal), (unit.at[slot], units[d])], out_sem.at[slot])
    for copy in pending[0] + pending[1] + outs:
        copy.wait()


def prep_kernel(unit, chips, me_ref, from_ref, to_ref, slot_ref, sus_ref, rate_ref,
                f_ref, t_ref, ratio_ref, k_ref, cnt_ref):
    half = ratio_ref.shape[0]
    groups = half // GROUP
    me = me_ref[0]
    start = (me & 1) * half
    flip = me * unit
    bits = unit.bit_length() - 1
    slot = columns([slot_ref[...].astype(jnp.float32)])

    square = (LANES, LANES)
    before = lax.broadcasted_iota(jnp.int32, square, 0) < lax.broadcasted_iota(jnp.int32, square, 1)
    before = jnp.where(before, 1.0, 0.0).astype(jnp.bfloat16)
    lane = lax.broadcasted_iota(jnp.int32, (1, LANES), 1).astype(jnp.float32)
    slots = lax.broadcasted_iota(jnp.int32, (GROUP * LANES, LANES), 0).astype(jnp.float32)
    cnt_ref[...] = jnp.zeros_like(cnt_ref)

    def place(bus_ref, row):
        bus = jnp.concatenate([bus_ref[pl.ds(row + i, 1), :] for i in range(GROUP)], 1)
        rel = lookup(slot, bus)[0].astype(jnp.int32) ^ flip
        chip = rel >> (bits + 1)
        core = (rel >> bits) & 1
        return chip, (rel & (unit - 1)) + (core * chips + chip) * unit

    def group(g, carry):
        f_chip, f = place(from_ref, start + g * GROUP)
        t_chip, t = place(to_ref, start + g * GROUP)
        first = jnp.where(jnp.maximum(f_chip, t_chip) < chips - LATE, 1.0, 0.0)
        tile = lambda a, i: a[:, i * LANES:(i + 1) * LANES]
        flags = jnp.concatenate([tile(first, i) for i in range(GROUP)]
                                + [jnp.zeros((8 - GROUP, LANES), jnp.float32)], 0)
        ahead = jnp.dot(flags.astype(jnp.bfloat16), before, preferred_element_type=jnp.float32)
        sums = jnp.sum(flags, axis=1, keepdims=True)
        count = sum(sums[i:i + 1] for i in range(GROUP))
        offset = jnp.zeros((1, 1), jnp.float32)
        total = jnp.zeros((16, GROUP * LANES), jnp.float32)
        for i in range(GROUP):
            front = offset + ahead[i:i + 1]
            rest = count + (lane + float(i * LANES)) - front
            goal = jnp.where(tile(first, i) > 0.5, front, rest)
            offset = offset + sums[i:i + 1]
            hot = jnp.where(slots == goal, 1.0, 0.0).astype(jnp.bfloat16)
            row = pl.ds(start + g * GROUP + i, 1)
            rows = [tile(f, i) >> 7, tile(f, i) & 127, tile(t, i) >> 7, tile(t, i) & 127]
            rows = [r.astype(jnp.float32) for r in rows]
            rows += [p.astype(jnp.float32) for p in split(sus_ref[row, :] / rate_ref[row, :], 3)]
            rows += [jnp.full((1, LANES), float(i)), lane] + [jnp.zeros((1, LANES), jnp.float32)] * 7
            values = jnp.concatenate(rows, 0).astype(jnp.bfloat16)
            total += lax.dot_general(values, hot, (((1,), (1,)), ((), ())), preferred_element_type=jnp.float32)
        for i in range(GROUP):
            out = pl.ds(i * groups + g, 1)
            part = total[:, i * LANES:(i + 1) * LANES]
            f_ref[out, :] = (part[0:1] * 128.0 + part[1:2]).astype(jnp.int32)
            t_ref[out, :] = (part[2:3] * 128.0 + part[3:4]).astype(jnp.int32)
            ratio_ref[out, :] = part[4:5] + part[5:6] + part[6:7]
            origin = ((start + g * GROUP) * LANES).astype(jnp.float32)
            k_ref[out, :] = part[7:8] * 128.0 + part[8:9] + origin
        blocks = jnp.broadcast_to(count, (1, LANES)).astype(jnp.int32) >> 7
        cnt_ref[...] = jnp.where(lane == g.astype(jnp.float32), blocks, cnt_ref[...])
        return carry

    lax.fori_loop(0, half // GROUP, group, 0)


def join_kernel(_, *refs):
    pieces, (out_ref, sem) = refs[:-2], refs[-2:]
    unit = pieces[0].shape[0]
    for copy in stage([(p, out_ref.at[pl.ds(i * unit, unit)]) for i, p in enumerate(pieces)], sem):
        copy.wait()


def worst_kernel(late, me_ref, f_ref, t_ref, cnt_ref, ratio_ref, k_ref, state_ref, *rest):
    if late:
        best_ref, *rest = rest
    pieces, (out_ref, table, f_s, t_s, cnt_s, best, diff, sem) = rest[:2 * late + 2], rest[2 * late + 2:]
    half = f_ref.shape[0]
    groups = half // GROUP
    side = [pl.ds(0, half // 2), pl.ds(half // 2, half // 2)]
    main, spare = side[late], side[1 - late]
    pairs = [(cnt_ref, cnt_s), (f_ref.at[main], f_s.at[main]), (t_ref.at[main], t_s.at[main])]
    row = 0
    for own, other in zip(pieces[::2], pieces[1::2]):
        size = own.shape[0]
        pairs += [(own, table.at[pl.ds(row, size)]),
                  (other, table.at[pl.ds(table.shape[0] // 2 + row, size)])]
        row += size
    copies = stage(pairs, sem)
    ids = state_ref[6, pl.ds(me_ref[0] >> 1, 1), :]
    best[...] = best_ref[...] if late else jnp.zeros_like(best)
    for copy in copies:
        copy.wait()
    bound = cnt_s[0, 0]
    for g in range(1, groups):
        bound = jnp.minimum(bound, cnt_s[0, g]) if late else jnp.maximum(bound, cnt_s[0, g])

    @pl.when(bound < GROUP // 2 if late else bound > GROUP // 2)
    def _():
        for copy in stage([(f_ref.at[spare], f_s.at[spare]), (t_ref.at[spare], t_s.at[spare])], sem):
            copy.wait()

    def group(g, carry):
        def block(i, carry):
            b = i * groups + g
            for j in range(LANES):
                diff[pl.ds(j, 1), :] = table[pl.ds(f_s[b, j], 1), :] - table[pl.ds(t_s[b, j], 1), :]
            turn = diff[...]
            turn = turn - jnp.round(turn)
            square = turn * turn
            poly = SINE[4]
            for c in SINE[3::-1]:
                poly = poly * square + c
            scale = jnp.broadcast_to(ratio_ref[pl.ds(b, 1), :], (LANES, LANES)).T
            branch = jnp.broadcast_to(k_ref[pl.ds(b, 1), :], (LANES, LANES)).T
            load = jnp.where(branch == ids, 0.0, jnp.abs(turn * poly) * scale)
            best[...] = jnp.maximum(best[...], jnp.max(load.reshape(LANES // 8, 8, LANES), axis=0))
            return carry

        return lax.fori_loop(cnt_s[0, g] if late else 0, GROUP if late else cnt_s[0, g], block, carry)

    lax.fori_loop(0, groups, group, 0)
    out_ref[...] = jnp.max(best[...], axis=0, keepdims=True) if late else best[...]


def per_device(
    outages, branch_from, branch_to, bus_slot, susceptance, charging, rating, base_angles, zinv
):
    n_col = lax.axis_size("col")
    buses, cols = zinv.shape
    own = outages.shape[0]
    total = own * n_col
    blocks = total // LANES
    chips = n_col // 2
    assert own * 2 == LANES and cols // LANES <= blocks and chips & (chips - 1) == 0 and chips > 2
    me = lax.axis_index("col")
    where = me[None]
    tab = lambda a: a.reshape(-1, LANES)
    from2, to2, slot2, sus2, chg2, rate2, base2 = map(
        tab, (branch_from, branch_to, bus_slot, susceptance, charging, rating, base_angles)
    )
    i32 = lambda *s: jax.ShapeDtypeStruct(s, jnp.int32)
    f32 = lambda *s: jax.ShapeDtypeStruct(s, jnp.float32)

    flat = zinv.reshape(buses // 8, 8, cols // LANES, LANES).transpose(0, 2, 1, 3).reshape(-1, LANES)
    ids = lax.dynamic_update_slice(jnp.zeros((total,), jnp.int32), outages, (me * own,))
    ids = lax.psum(ids[None], "col")

    width = cols // LANES
    like = lambda a: pltpu.VMEM(a.shape, a.dtype)
    row_shape = (2, width * LANES, LANES)
    state, picks, rows = pl.pallas_call(
        functools.partial(ends_kernel, width),
        name="ends",
        out_shape=[f32(8, blocks, LANES), f32(3 * blocks, LANES), f32(blocks, *row_shape)],
        in_specs=[SMEM, VMEM] + [ANY] * 7,
        out_specs=[VMEM] * 2 + [ANY],
        scratch_shapes=[like(from2), like(to2), like(slot2), like(sus2), like(chg2), like(base2), like(flat),
                        pltpu.VMEM((2 * blocks, LANES), jnp.int32), pltpu.SMEM((2 * blocks, LANES), jnp.int32),
                        pltpu.VMEM((2,) + row_shape, jnp.float32), pltpu.SemaphoreType.DMA((6,)),
                        pltpu.SemaphoreType.DMA((2,)), pltpu.SemaphoreType.DMA((CHUNKS,))],
        compiler_params=params(60),
    )(where, ids, from2, to2, slot2, sus2, chg2, base2, flat)

    swap = lambda a, m: lax.ppermute(a, "col", [(i, i ^ m) for i in range(n_col)])
    step = 1
    terms = [picks]
    while step < n_col:
        picks = sum(terms)
        terms = [picks] + [swap(picks, m * step) for m in range(1, min(4, n_col // step))]
        step *= 4

    injections, deviation, *units = pl.pallas_call(
        functools.partial(spread_kernel, chips, len(terms)),
        name="spread",
        out_shape=[f32(2, blocks, LANES), f32(total, cols)] + [f32(cols, LANES)] * chips,
        in_specs=[SMEM] + [ANY] * (2 + len(terms)),
        out_specs=[ANY] * (2 + chips),
        scratch_shapes=[like(state), pltpu.VMEM((len(terms),) + picks.shape, jnp.float32),
                        pltpu.VMEM((2, blocks, LANES), jnp.float32), like(rows),
                        pltpu.VMEM((2, LANES, cols), jnp.float32), pltpu.VMEM((2, cols, LANES), jnp.float32),
                        pltpu.SemaphoreType.DMA((1 + len(terms),)), pltpu.SemaphoreType.DMA((chips,)),
                        pltpu.SemaphoreType.DMA((2, 2))],
        compiler_params=params(52),
    )(where, state, rows, *terms)

    half = branch_from.shape[0] // LANES // 2
    f_rel, t_rel, ratio, k_rel, counts = pl.pallas_call(
        functools.partial(prep_kernel, cols, chips),
        name="prep",
        out_shape=[i32(half, LANES), i32(half, LANES), f32(half, LANES), f32(half, LANES),
                   i32(1, LANES)],
        in_specs=[SMEM] + [VMEM] * 5,
        out_specs=[VMEM] * 5,
        compiler_params=params(16),
    )(where, from2, to2, slot2, sus2, rate2)

    got = [units[0]] + [swap(units[d], 2 * d) for d in range(1, chips)]

    def join(after, pieces):
        packed = pl.pallas_call(
            join_kernel,
            name="join",
            out_shape=f32(len(pieces) * cols, LANES),
            in_specs=[ANY] * (1 + len(pieces)),
            out_specs=VMEM,
            scratch_shapes=[pltpu.SemaphoreType.DMA((len(pieces),))],
            compiler_params=params(16),
        )(after, *pieces)
        return [packed, swap(packed, 1)]

    def worst_of(level, *operands):
        return pl.pallas_call(
            functools.partial(worst_kernel, level),
            name=f"worst{level}",
            out_shape=f32(1 if level else 8, LANES),
            in_specs=[SMEM] + [ANY] * 3 + [VMEM] * (3 + level) + [ANY] * (len(operands) - level),
            out_specs=VMEM,
            scratch_shapes=[pltpu.VMEM((buses, LANES), jnp.float32), pltpu.SMEM(f_rel.shape, jnp.int32),
                            pltpu.SMEM(t_rel.shape, jnp.int32), pltpu.SMEM(counts.shape, jnp.int32),
                            pltpu.VMEM((8, LANES), jnp.float32), pltpu.VMEM((LANES, LANES), jnp.float32),
                            pltpu.SemaphoreType.DMA((3 + len(operands),))],
            compiler_params=params(16),
        )(where, f_rel, t_rel, counts, ratio, k_rel, state, *operands)

    early = join(counts, got[:-LATE])
    best = worst_of(0, *early)
    worst = worst_of(1, best, *early, *join(best, got[-LATE:]))
    mine = lambda a, b: lax.dynamic_slice(a, (jnp.int32(0),) * (a.ndim - len(b)) + b, a.shape[:1] + (1,) * (a.ndim - 2) + (own,))
    worst = jnp.maximum(mine(worst, ((me & 1) * own,)), mine(swap(worst, 1), ((me & 1) * own,))).reshape(own)
    inj = mine(injections, (me >> 1, (me & 1) * own)).reshape(2, own)
    return inj, deviation, worst


def solution(mesh):
    return jax.shard_map(
        per_device,
        mesh=mesh,
        in_specs=(P(("parts", "col")), P(), P(), P(), P(), P(), P(), P("parts"), P(None, "col")),
        out_specs=(P(None, ("parts", "col")), P("parts", "col"), P(("parts", "col"))),
        check_vma=False,
    )
```

```python
import functools
import math

import jax
import jax.numpy as jnp
from jax import lax
from jax.experimental import pallas as pl
from jax.experimental.pallas import tpu as pltpu
from jax.sharding import PartitionSpec as P

STEPS = 3
LANES = 128
LATE = 2
CHUNKS = 1
GROUP = 4
SINE = (3.1415926444, -5.1677100819, 2.5500775297, -0.5982913039, 0.0776576582)
VMEM = pl.BlockSpec(memory_space=pltpu.VMEM)
SMEM = pl.BlockSpec(memory_space=pltpu.SMEM)
ANY = pl.BlockSpec(memory_space=pl.ANY)


def params(mib):
    return pltpu.CompilerParams(vmem_limit_bytes=mib * 2**20)


def split(table, parts):
    out = []
    for _ in range(parts):
        piece = table.astype(jnp.bfloat16)
        out.append(piece)
        table = table - piece.astype(jnp.float32)
    return out


def columns(tables):
    return jnp.concatenate([jnp.concatenate(split(t.T, 3), 1) for t in tables], 0)


def lookup(turned, index):
    rows = turned.shape[1] // 3
    n = index.shape[1]
    hot = lax.broadcasted_iota(jnp.int32, (rows, n), 0) == (index >> 7)
    hot = jnp.where(hot, 1.0, 0.0).astype(jnp.bfloat16)
    picked = jnp.dot(turned, jnp.concatenate([hot] * 3, 0), preferred_element_type=jnp.float32)
    lane = lax.broadcasted_iota(jnp.int32, (LANES, n), 0) == (index & 127)
    return [jnp.sum(jnp.where(lane, picked[i:i + LANES], 0.0), axis=0, keepdims=True)
            for i in range(0, turned.shape[0], LANES)]


def newton(a_head, a_tail, self_head, cross, self_tail, bsus, hchg):
    inj_head = jnp.zeros_like(a_head)
    inj_tail = jnp.zeros_like(a_head)
    for step in range(1, STEPS + 1):
        level = step / STEPS
        end_head = a_head + self_head * inj_head + cross * inj_tail
        end_tail = a_tail + cross * inj_head + self_tail * inj_tail
        spread = end_head - end_tail
        sine_val = jnp.sin(spread)
        cosine_val = jnp.cos(spread)
        resid_head = inj_head - level * (bsus * sine_val + hchg * end_head)
        resid_tail = inj_tail - level * (-bsus * sine_val + hchg * end_tail)
        diag_term = bsus * cosine_val + hchg
        cross_term = -bsus * cosine_val
        jac_one = 1.0 - level * (diag_term * self_head + cross_term * cross)
        jac_two = -level * (diag_term * cross + cross_term * self_tail)
        jac_three = -level * (cross_term * self_head + diag_term * cross)
        jac_four = 1.0 - level * (cross_term * cross + diag_term * self_tail)
        determinant = jac_one * jac_four - jac_two * jac_three
        inj_head = inj_head - (jac_four * resid_head - jac_two * resid_tail) / determinant
        inj_tail = inj_tail - (jac_one * resid_tail - jac_three * resid_head) / determinant
    return inj_head, inj_tail


def addresses(row, width):
    return (row >> 3) * (8 * width) + (row & 7)


def stage(pairs, sem):
    copies = [pltpu.make_async_copy(src, dst, sem.at[i]) for i, (src, dst) in enumerate(pairs)]
    for copy in copies:
        copy.start()
    return copies


def ends_kernel(width, me_ref, ids_ref, from_ref, to_ref, slot_ref, sus_ref, chg_ref, base_ref, zinv_ref,
                state_ref, pick_ref, rows_ref, from_v, to_v, slot_v, sus_v, chg_v, base_v,
                zinv_v, ends_v, ends_s, rows, sem, out_sem, zinv_sem):
    total = ids_ref.shape[1]
    blocks = total // LANES
    first = me_ref[0] * width * LANES
    copies = stage([(from_ref, from_v), (to_ref, to_v), (slot_ref, slot_v), (sus_ref, sus_v),
                    (chg_ref, chg_v), (base_ref, base_v)], sem)
    part = zinv_v.shape[0] // CHUNKS
    cuts = [pl.ds(i * part, part) for i in range(CHUNKS)]
    zinv_copies = stage([(zinv_ref.at[c], zinv_v.at[c]) for c in cuts], zinv_sem)
    for copy in copies:
        copy.wait()
    branch = columns([from_v[...].astype(jnp.float32), to_v[...].astype(jnp.float32), sus_v[...], chg_v[...]])
    slot = columns([slot_v[...].astype(jnp.float32)])
    base = columns([base_v[...]])
    wide = min(total, 8 * LANES)
    for c in range(0, total, wide):
        ids = ids_ref[:, c:c + wide]
        f, t, sus, chg = lookup(branch, ids)
        ends, = lookup(slot, jnp.concatenate([f, t], 1).astype(jnp.int32))
        ends = ends.astype(jnp.int32)
        angle, = lookup(base, ends)
        place = addresses(ends, width)
        local = (ends - first).astype(jnp.float32)
        known = (angle[:, :wide], angle[:, wide:], sus, chg, local[:, :wide], local[:, wide:],
                 ids.astype(jnp.float32))
        for b in range(wide // LANES):
            row = slice(c // LANES + b, c // LANES + b + 1)
            at = slice(b * LANES, (b + 1) * LANES)
            ends_v[row, :] = place[:, at]
            ends_v[slice(blocks + row.start, blocks + row.stop), :] = place[:, b * LANES + wide:(b + 1) * LANES + wide]
            for i, value in enumerate(known):
                state_ref[i, row, :] = value[:, at]
    copy = pltpu.make_async_copy(ends_v, ends_s, sem.at[0])
    copy.start()
    for t in range(width):
        state_ref[7, t:t + 1, :] = base_v[pl.ds(me_ref[0] * width + t, 1), :]
    copy.wait()
    for copy in zinv_copies:
        copy.wait()

    def fetch(b, slot):
        for o in range(LANES):
            at = pl.ds(o * width, width)
            rows[slot, 0, at, :] = zinv_v[pl.ds(ends_s[b, o], width, stride=8), :]
            rows[slot, 1, at, :] = zinv_v[pl.ds(ends_s[blocks + b, o], width, stride=8), :]

    def choose(b, slot):
        square = (LANES, LANES)
        at_h = jnp.broadcast_to(state_ref[4, pl.ds(b, 1), :], square).T
        at_t = jnp.broadcast_to(state_ref[5, pl.ds(b, 1), :], square).T
        lane = lax.broadcasted_iota(jnp.int32, square, 1).astype(jnp.float32)
        hh = ht = tt = jnp.zeros(square, jnp.float32)
        for t in range(width):
            is_h = at_h == lane + float(t * LANES)
            is_t = at_t == lane + float(t * LANES)
            piece = pl.ds(t, LANES, stride=width)
            row_h, row_t = rows[slot, 0, piece, :], rows[slot, 1, piece, :]
            hh = jnp.where(is_h, row_h, hh)
            ht = jnp.where(is_t, row_h, ht)
            tt = jnp.where(is_t, row_t, tt)
        for i, pick in enumerate((hh, ht, tt)):
            pick_ref[pl.ds(i * blocks + b, 1), :] = jnp.sum(pick.T, axis=0, keepdims=True)

    def send(b, slot):
        return pltpu.make_async_copy(rows.at[slot], rows_ref.at[b], out_sem.at[slot])

    def pair(i, carry):
        for slot in (0, 1):
            b = 2 * i + slot

            @pl.when(i > 0)
            def _():
                send(b - 2, slot).wait()

            fetch(b, slot)
            choose(jnp.maximum(b - 1, 0), 1 - slot)
            send(b, slot).start()
        return carry

    rows[1] = jnp.zeros_like(rows[1])
    lax.fori_loop(0, blocks // 2, pair, 0)
    choose(blocks - 1, 1)
    for slot in (0, 1):
        send(blocks - 2 + slot, slot).wait()


def spread_kernel(chips, terms, me_ref, state_ref, rows_ref, *rest):
    pick_refs, (inj_ref, dev_ref, *rest) = rest[:terms], rest[terms:]
    units, (state, pick, inj, rows, dev, unit, in_sem, row_sem, out_sem) = rest[:chips], rest[chips:]
    blocks, width = chips, dev.shape[2] // LANES
    me = me_ref[0]
    small = stage([(state_ref, state)] + [(p, pick.at[i]) for i, p in enumerate(pick_refs)], in_sem)
    whole = [pltpu.make_async_copy(rows_ref.at[(me >> 1) ^ d], rows.at[d], row_sem.at[d]) for d in range(chips)]
    for copy in whole:
        copy.start()
    for copy in small:
        copy.wait()
    picks = sum(pick[i] for i in range(terms))
    inj_h, inj_t = newton(state[0], state[1], picks[:blocks], picks[blocks:2 * blocks], picks[2 * blocks:],
                          state[2], state[3])
    inj[0] = inj_h
    inj[1] = inj_t
    outs = [pltpu.make_async_copy(inj, inj_ref, in_sem.at[0])]
    outs[0].start()
    order = list(range(chips // 2, chips)) + list(range(chips // 2))
    pending = [None, None]
    for i, d in enumerate(order):
        slot = i % 2
        blk = (me >> 1) ^ d
        scale_h = jnp.broadcast_to(inj[0, pl.ds(blk, 1), :], (LANES, LANES)).T
        scale_t = jnp.broadcast_to(inj[1, pl.ds(blk, 1), :], (LANES, LANES)).T
        whole[d].wait()
        for copy in pending[slot] or ():
            copy.wait()
        for t in range(width):
            at = slice(t * LANES, (t + 1) * LANES)
            piece = pl.ds(t, LANES, stride=width)
            value = scale_h * rows[d, 0, piece, :] + scale_t * rows[d, 1, piece, :]
            dev[slot, :, at] = value
            unit[slot, at, :] = ((state[7, t:t + 1, :] + value) * (1.0 / math.pi)).T
        goal = dev_ref.at[pl.ds(pl.multiple_of(blk * LANES, LANES), LANES)]
        pending[slot] = stage([(dev.at[slot], goal), (unit.at[slot], units[d])], out_sem.at[slot])
    for copy in pending[0] + pending[1] + outs:
        copy.wait()


def prep_kernel(unit, chips, me_ref, from_ref, to_ref, slot_ref, sus_ref, rate_ref,
                f_ref, t_ref, ratio_ref, k_ref, cnt_ref):
    half = ratio_ref.shape[0]
    groups = half // GROUP
    me = me_ref[0]
    start = (me & 1) * half
    flip = me * unit
    bits = unit.bit_length() - 1
    slot = columns([slot_ref[...].astype(jnp.float32)])

    square = (LANES, LANES)
    before = lax.broadcasted_iota(jnp.int32, square, 0) < lax.broadcasted_iota(jnp.int32, square, 1)
    before = jnp.where(before, 1.0, 0.0).astype(jnp.bfloat16)
    lane = lax.broadcasted_iota(jnp.int32, (1, LANES), 1).astype(jnp.float32)
    slots = lax.broadcasted_iota(jnp.int32, (GROUP * LANES, LANES), 0).astype(jnp.float32)
    cnt_ref[...] = jnp.zeros_like(cnt_ref)

    def place(bus_ref, row):
        bus = jnp.concatenate([bus_ref[pl.ds(row + i, 1), :] for i in range(GROUP)], 1)
        rel = lookup(slot, bus)[0].astype(jnp.int32) ^ flip
        chip = rel >> (bits + 1)
        core = (rel >> bits) & 1
        return chip, (rel & (unit - 1)) + (core * chips + chip) * unit

    def group(g, carry):
        f_chip, f = place(from_ref, start + g * GROUP)
        t_chip, t = place(to_ref, start + g * GROUP)
        first = jnp.where(jnp.maximum(f_chip, t_chip) < chips - LATE, 1.0, 0.0)
        tile = lambda a, i: a[:, i * LANES:(i + 1) * LANES]
        flags = jnp.concatenate([tile(first, i) for i in range(GROUP)]
                                + [jnp.zeros((8 - GROUP, LANES), jnp.float32)], 0)
        ahead = jnp.dot(flags.astype(jnp.bfloat16), before, preferred_element_type=jnp.float32)
        sums = jnp.sum(flags, axis=1, keepdims=True)
        count = sum(sums[i:i + 1] for i in range(GROUP))
        offset = jnp.zeros((1, 1), jnp.float32)
        total = jnp.zeros((16, GROUP * LANES), jnp.float32)
        for i in range(GROUP):
            front = offset + ahead[i:i + 1]
            rest = count + (lane + float(i * LANES)) - front
            goal = jnp.where(tile(first, i) > 0.5, front, rest)
            offset = offset + sums[i:i + 1]
            hot = jnp.where(slots == goal, 1.0, 0.0).astype(jnp.bfloat16)
            row = pl.ds(start + g * GROUP + i, 1)
            rows = [tile(f, i) >> 7, tile(f, i) & 127, tile(t, i) >> 7, tile(t, i) & 127]
            rows = [r.astype(jnp.float32) for r in rows]
            rows += [p.astype(jnp.float32) for p in split(sus_ref[row, :] / rate_ref[row, :], 3)]
            rows += [jnp.full((1, LANES), float(i)), lane] + [jnp.zeros((1, LANES), jnp.float32)] * 7
            values = jnp.concatenate(rows, 0).astype(jnp.bfloat16)
            total += lax.dot_general(values, hot, (((1,), (1,)), ((), ())), preferred_element_type=jnp.float32)
        for i in range(GROUP):
            out = pl.ds(i * groups + g, 1)
            part = total[:, i * LANES:(i + 1) * LANES]
            f_ref[out, :] = (part[0:1] * 128.0 + part[1:2]).astype(jnp.int32)
            t_ref[out, :] = (part[2:3] * 128.0 + part[3:4]).astype(jnp.int32)
            ratio_ref[out, :] = part[4:5] + part[5:6] + part[6:7]
            origin = ((start + g * GROUP) * LANES).astype(jnp.float32)
            k_ref[out, :] = part[7:8] * 128.0 + part[8:9] + origin
        blocks = jnp.broadcast_to(count, (1, LANES)).astype(jnp.int32) >> 7
        cnt_ref[...] = jnp.where(lane == g.astype(jnp.float32), blocks, cnt_ref[...])
        return carry

    lax.fori_loop(0, half // GROUP, group, 0)


def join_kernel(_, *refs):
    pieces, (out_ref, sem) = refs[:-2], refs[-2:]
    unit = pieces[0].shape[0]
    for copy in stage([(p, out_ref.at[pl.ds(i * unit, unit)]) for i, p in enumerate(pieces)], sem):
        copy.wait()


def worst_kernel(late, me_ref, f_ref, t_ref, cnt_ref, ratio_ref, k_ref, state_ref, *rest):
    if late:
        best_ref, *rest = rest
    pieces, (out_ref, table, f_s, t_s, cnt_s, best, diff, sem) = rest[:2 * late + 2], rest[2 * late + 2:]
    half = f_ref.shape[0]
    groups = half // GROUP
    side = [pl.ds(0, half // 2), pl.ds(half // 2, half // 2)]
    main, spare = side[late], side[1 - late]
    pairs = [(cnt_ref, cnt_s), (f_ref.at[main], f_s.at[main]), (t_ref.at[main], t_s.at[main])]
    row = 0
    for own, other in zip(pieces[::2], pieces[1::2]):
        size = own.shape[0]
        pairs += [(own, table.at[pl.ds(row, size)]),
                  (other, table.at[pl.ds(table.shape[0] // 2 + row, size)])]
        row += size
    copies = stage(pairs, sem)
    ids = state_ref[6, pl.ds(me_ref[0] >> 1, 1), :]
    best[...] = best_ref[...] if late else jnp.zeros_like(best)
    for copy in copies:
        copy.wait()
    bound = cnt_s[0, 0]
    for g in range(1, groups):
        bound = jnp.minimum(bound, cnt_s[0, g]) if late else jnp.maximum(bound, cnt_s[0, g])

    @pl.when(bound < GROUP // 2 if late else bound > GROUP // 2)
    def _():
        for copy in stage([(f_ref.at[spare], f_s.at[spare]), (t_ref.at[spare], t_s.at[spare])], sem):
            copy.wait()

    def group(g, carry):
        def block(i, carry):
            b = i * groups + g
            for j in range(LANES):
                diff[pl.ds(j, 1), :] = table[pl.ds(f_s[b, j], 1), :] - table[pl.ds(t_s[b, j], 1), :]
            turn = diff[...]
            turn = turn - jnp.round(turn)
            square = turn * turn
            poly = SINE[4]
            for c in SINE[3::-1]:
                poly = poly * square + c
            scale = jnp.broadcast_to(ratio_ref[pl.ds(b, 1), :], (LANES, LANES)).T
            branch = jnp.broadcast_to(k_ref[pl.ds(b, 1), :], (LANES, LANES)).T
            load = jnp.where(branch == ids, 0.0, jnp.abs(turn * poly) * scale)
            best[...] = jnp.maximum(best[...], jnp.max(load.reshape(LANES // 8, 8, LANES), axis=0))
            return carry

        return lax.fori_loop(cnt_s[0, g] if late else 0, GROUP if late else cnt_s[0, g], block, carry)

    lax.fori_loop(0, groups, group, 0)
    out_ref[...] = jnp.max(best[...], axis=0, keepdims=True) if late else best[...]


def per_device(
    outages, branch_from, branch_to, bus_slot, susceptance, charging, rating, base_angles, zinv
):
    n_col = lax.axis_size("col")
    buses, cols = zinv.shape
    own = outages.shape[0]
    total = own * n_col
    blocks = total // LANES
    chips = n_col // 2
    assert own * 2 == LANES and cols // LANES <= blocks and chips & (chips - 1) == 0 and chips > 2
    me = lax.axis_index("col")
    where = me[None]
    tab = lambda a: a.reshape(-1, LANES)
    from2, to2, slot2, sus2, chg2, rate2, base2 = map(
        tab, (branch_from, branch_to, bus_slot, susceptance, charging, rating, base_angles)
    )
    i32 = lambda *s: jax.ShapeDtypeStruct(s, jnp.int32)
    f32 = lambda *s: jax.ShapeDtypeStruct(s, jnp.float32)

    flat = zinv.reshape(buses // 8, 8, cols // LANES, LANES).transpose(0, 2, 1, 3).reshape(-1, LANES)
    ids = lax.dynamic_update_slice(jnp.zeros((total,), jnp.int32), outages, (me * own,))
    ids = lax.psum(ids[None], "col")

    width = cols // LANES
    like = lambda a: pltpu.VMEM(a.shape, a.dtype)
    row_shape = (2, width * LANES, LANES)
    state, picks, rows = pl.pallas_call(
        functools.partial(ends_kernel, width),
        name="ends",
        out_shape=[f32(8, blocks, LANES), f32(3 * blocks, LANES), f32(blocks, *row_shape)],
        in_specs=[SMEM, VMEM] + [ANY] * 7,
        out_specs=[VMEM] * 2 + [ANY],
        scratch_shapes=[like(from2), like(to2), like(slot2), like(sus2), like(chg2), like(base2), like(flat),
                        pltpu.VMEM((2 * blocks, LANES), jnp.int32), pltpu.SMEM((2 * blocks, LANES), jnp.int32),
                        pltpu.VMEM((2,) + row_shape, jnp.float32), pltpu.SemaphoreType.DMA((6,)),
                        pltpu.SemaphoreType.DMA((2,)), pltpu.SemaphoreType.DMA((CHUNKS,))],
        compiler_params=params(60),
    )(where, ids, from2, to2, slot2, sus2, chg2, base2, flat)

    swap = lambda a, m: lax.ppermute(a, "col", [(i, i ^ m) for i in range(n_col)])
    step = 1
    terms = [picks]
    while step < n_col:
        picks = sum(terms)
        terms = [picks] + [swap(picks, m * step) for m in range(1, min(4, n_col // step))]
        step *= 4

    nearby = state + jnp.minimum(me, 0).astype(jnp.float32)
    injections, deviation, *units = pl.pallas_call(
        functools.partial(spread_kernel, chips, len(terms)),
        name="spread",
        out_shape=[f32(2, blocks, LANES), f32(total, cols)] + [f32(cols, LANES)] * chips,
        in_specs=[SMEM] + [ANY] * (2 + len(terms)),
        out_specs=[ANY] * (2 + chips),
        scratch_shapes=[like(state), pltpu.VMEM((len(terms),) + picks.shape, jnp.float32),
                        pltpu.VMEM((2, blocks, LANES), jnp.float32), like(rows),
                        pltpu.VMEM((2, LANES, cols), jnp.float32), pltpu.VMEM((2, cols, LANES), jnp.float32),
                        pltpu.SemaphoreType.DMA((1 + len(terms),)), pltpu.SemaphoreType.DMA((chips,)),
                        pltpu.SemaphoreType.DMA((2, 2))],
        compiler_params=params(52),
    )(where, nearby, rows, *terms)

    half = branch_from.shape[0] // LANES // 2
    f_rel, t_rel, ratio, k_rel, counts = pl.pallas_call(
        functools.partial(prep_kernel, cols, chips),
        name="prep",
        out_shape=[i32(half, LANES), i32(half, LANES), f32(half, LANES), f32(half, LANES),
                   i32(1, LANES)],
        in_specs=[SMEM] + [VMEM] * 5,
        out_specs=[VMEM] * 5,
        compiler_params=params(16),
    )(where, from2, to2, slot2, sus2, rate2)

    got = [units[0]] + [swap(units[d], 2 * d) for d in range(1, chips)]

    def join(after, pieces):
        packed = pl.pallas_call(
            join_kernel,
            name="join",
            out_shape=f32(len(pieces) * cols, LANES),
            in_specs=[ANY] * (1 + len(pieces)),
            out_specs=VMEM,
            scratch_shapes=[pltpu.SemaphoreType.DMA((len(pieces),))],
            compiler_params=params(16),
        )(after, *pieces)
        return [packed, swap(packed, 1)]

    def worst_of(level, *operands):
        return pl.pallas_call(
            functools.partial(worst_kernel, level),
            name=f"worst{level}",
            out_shape=f32(1 if level else 8, LANES),
            in_specs=[SMEM] + [ANY] * 3 + [VMEM] * (3 + level) + [ANY] * (len(operands) - level),
            out_specs=VMEM,
            scratch_shapes=[pltpu.VMEM((buses, LANES), jnp.float32), pltpu.SMEM(f_rel.shape, jnp.int32),
                            pltpu.SMEM(t_rel.shape, jnp.int32), pltpu.SMEM(counts.shape, jnp.int32),
                            pltpu.VMEM((8, LANES), jnp.float32), pltpu.VMEM((LANES, LANES), jnp.float32),
                            pltpu.SemaphoreType.DMA((3 + len(operands),))],
            compiler_params=params(16),
        )(where, f_rel, t_rel, counts, ratio, k_rel, state, *operands)

    early = join(counts, got[:-LATE])
    best = worst_of(0, *early)
    worst = worst_of(1, best, *early, *join(best, got[-LATE:]))
    mine = lambda a, b: lax.dynamic_slice(a, (jnp.int32(0),) * (a.ndim - len(b)) + b, a.shape[:1] + (1,) * (a.ndim - 2) + (own,))
    worst = jnp.maximum(mine(worst, ((me & 1) * own,)), mine(swap(worst, 1), ((me & 1) * own,))).reshape(own)
    inj = mine(injections, (me >> 1, (me & 1) * own)).reshape(2, own)
    return inj, deviation, worst


def solution(mesh):
    return jax.shard_map(
        per_device,
        mesh=mesh,
        in_specs=(P(("parts", "col")), P(), P(), P(), P(), P(), P(), P("parts"), P(None, "col")),
        out_specs=(P(None, ("parts", "col")), P("parts", "col"), P(("parts", "col"))),
        check_vma=False,
    )
```

```python
import functools
import math

import jax
import jax.numpy as jnp
from jax import lax
from jax.experimental import pallas as pl
from jax.experimental.pallas import tpu as pltpu
from jax.sharding import PartitionSpec as P

STEPS = 3
LANES = 128
SPARE = 64
LATE = 2
CHUNKS = 1
GROUP = 4
SINE = (3.1415926444, -5.1677100819, 2.5500775297, -0.5982913039, 0.0776576582)
VMEM = pl.BlockSpec(memory_space=pltpu.VMEM)
SMEM = pl.BlockSpec(memory_space=pltpu.SMEM)
ANY = pl.BlockSpec(memory_space=pl.ANY)


def params(mib):
    return pltpu.CompilerParams(vmem_limit_bytes=mib * 2**20)


def split(table, parts):
    out = []
    for _ in range(parts):
        piece = table.astype(jnp.bfloat16)
        out.append(piece)
        table = table - piece.astype(jnp.float32)
    return out


def columns(tables):
    return jnp.concatenate([jnp.concatenate(split(t.T, 3), 1) for t in tables], 0)


def lookup(turned, index):
    rows = turned.shape[1] // 3
    n = index.shape[1]
    hot = lax.broadcasted_iota(jnp.int32, (rows, n), 0) == (index >> 7)
    hot = jnp.where(hot, 1.0, 0.0).astype(jnp.bfloat16)
    picked = jnp.dot(turned, jnp.concatenate([hot] * 3, 0), preferred_element_type=jnp.float32)
    lane = lax.broadcasted_iota(jnp.int32, (LANES, n), 0) == (index & 127)
    return [jnp.sum(jnp.where(lane, picked[i:i + LANES], 0.0), axis=0, keepdims=True)
            for i in range(0, turned.shape[0], LANES)]


def newton(a_head, a_tail, self_head, cross, self_tail, bsus, hchg):
    inj_head = jnp.zeros_like(a_head)
    inj_tail = jnp.zeros_like(a_head)
    for step in range(1, STEPS + 1):
        level = step / STEPS
        end_head = a_head + self_head * inj_head + cross * inj_tail
        end_tail = a_tail + cross * inj_head + self_tail * inj_tail
        spread = end_head - end_tail
        sine_val = jnp.sin(spread)
        cosine_val = jnp.cos(spread)
        resid_head = inj_head - level * (bsus * sine_val + hchg * end_head)
        resid_tail = inj_tail - level * (-bsus * sine_val + hchg * end_tail)
        diag_term = bsus * cosine_val + hchg
        cross_term = -bsus * cosine_val
        jac_one = 1.0 - level * (diag_term * self_head + cross_term * cross)
        jac_two = -level * (diag_term * cross + cross_term * self_tail)
        jac_three = -level * (cross_term * self_head + diag_term * cross)
        jac_four = 1.0 - level * (cross_term * cross + diag_term * self_tail)
        determinant = jac_one * jac_four - jac_two * jac_three
        inj_head = inj_head - (jac_four * resid_head - jac_two * resid_tail) / determinant
        inj_tail = inj_tail - (jac_one * resid_tail - jac_three * resid_head) / determinant
    return inj_head, inj_tail


def addresses(row, width):
    return (row >> 3) * (8 * width) + (row & 7)


def stage(pairs, sem):
    copies = [pltpu.make_async_copy(src, dst, sem.at[i]) for i, (src, dst) in enumerate(pairs)]
    for copy in copies:
        copy.start()
    return copies


def ends_kernel(width, me_ref, ids_ref, from_ref, to_ref, slot_ref, sus_ref, chg_ref, base_ref, zinv_ref,
                state_ref, pick_ref, rows_ref, from_v, to_v, slot_v, sus_v, chg_v, base_v,
                zinv_v, ends_v, ends_s, rows, sem, out_sem, zinv_sem):
    total = ids_ref.shape[1]
    blocks = total // LANES
    first = me_ref[0] * width * LANES
    copies = stage([(from_ref, from_v), (to_ref, to_v), (slot_ref, slot_v), (sus_ref, sus_v),
                    (chg_ref, chg_v), (base_ref, base_v)], sem)
    part = zinv_ref.shape[0] // CHUNKS
    cuts = [pl.ds(i * part, part) for i in range(CHUNKS)]
    zinv_copies = stage([(zinv_ref.at[c], zinv_v.at[c]) for c in cuts], zinv_sem)
    for copy in copies:
        copy.wait()
    branch = columns([from_v[...].astype(jnp.float32), to_v[...].astype(jnp.float32), sus_v[...], chg_v[...]])
    slot = columns([slot_v[...].astype(jnp.float32)])
    base = columns([base_v[...]])
    wide = min(total, 8 * LANES)
    for c in range(0, total, wide):
        ids = ids_ref[:, c:c + wide]
        f, t, sus, chg = lookup(branch, ids)
        ends, = lookup(slot, jnp.concatenate([f, t], 1).astype(jnp.int32))
        ends = ends.astype(jnp.int32)
        angle, = lookup(base, ends)
        place = addresses(ends, width)
        local = (ends - first).astype(jnp.float32)
        known = (angle[:, :wide], angle[:, wide:], sus, chg, local[:, :wide], local[:, wide:],
                 ids.astype(jnp.float32))
        for b in range(wide // LANES):
            row = slice(c // LANES + b, c // LANES + b + 1)
            at = slice(b * LANES, (b + 1) * LANES)
            ends_v[row, :] = place[:, at]
            ends_v[slice(blocks + row.start, blocks + row.stop), :] = place[:, b * LANES + wide:(b + 1) * LANES + wide]
            for i, value in enumerate(known):
                state_ref[i, row, :] = value[:, at]
    copy = pltpu.make_async_copy(ends_v, ends_s, sem.at[0])
    copy.start()
    for t in range(width):
        state_ref[7, t:t + 1, :] = base_v[pl.ds(me_ref[0] * width + t, 1), :]
    copy.wait()
    for copy in zinv_copies:
        copy.wait()

    def fetch(b, slot):
        for o in range(LANES):
            at = pl.ds(o * width, width)
            rows[slot, 0, at, :] = zinv_v[pl.ds(ends_s[b, o], width, stride=8), :]
            rows[slot, 1, at, :] = zinv_v[pl.ds(ends_s[blocks + b, o], width, stride=8), :]

    def choose(b, slot):
        square = (LANES, LANES)
        at_h = jnp.broadcast_to(state_ref[4, pl.ds(b, 1), :], square).T
        at_t = jnp.broadcast_to(state_ref[5, pl.ds(b, 1), :], square).T
        lane = lax.broadcasted_iota(jnp.int32, square, 1).astype(jnp.float32)
        hh = ht = tt = jnp.zeros(square, jnp.float32)
        for t in range(width):
            is_h = at_h == lane + float(t * LANES)
            is_t = at_t == lane + float(t * LANES)
            piece = pl.ds(t, LANES, stride=width)
            row_h, row_t = rows[slot, 0, piece, :], rows[slot, 1, piece, :]
            hh = jnp.where(is_h, row_h, hh)
            ht = jnp.where(is_t, row_h, ht)
            tt = jnp.where(is_t, row_t, tt)
        for i, pick in enumerate((hh, ht, tt)):
            pick_ref[pl.ds(i * blocks + b, 1), :] = jnp.sum(pick.T, axis=0, keepdims=True)

    def send(b, slot):
        return pltpu.make_async_copy(rows.at[slot], rows_ref.at[b], out_sem.at[slot])

    def pair(i, carry):
        for slot in (0, 1):
            b = 2 * i + slot

            @pl.when(i > 0)
            def _():
                send(b - 2, slot).wait()

            fetch(b, slot)
            choose(jnp.maximum(b - 1, 0), 1 - slot)
            send(b, slot).start()
        return carry

    rows[1] = jnp.zeros_like(rows[1])
    lax.fori_loop(0, blocks // 2, pair, 0)
    choose(blocks - 1, 1)
    for slot in (0, 1):
        send(blocks - 2 + slot, slot).wait()


def spread_kernel(chips, terms, me_ref, state_ref, rows_ref, *rest):
    pick_refs, (inj_ref, dev_ref, *rest) = rest[:terms], rest[terms:]
    units, (state, pick, inj, rows, dev, unit, in_sem, row_sem, out_sem) = rest[:chips], rest[chips:]
    blocks, width = chips, dev.shape[2] // LANES
    me = me_ref[0]
    small = stage([(state_ref, state)] + [(p, pick.at[i]) for i, p in enumerate(pick_refs)], in_sem)
    whole = [pltpu.make_async_copy(rows_ref.at[(me >> 1) ^ d], rows.at[d], row_sem.at[d]) for d in range(chips)]
    for copy in whole:
        copy.start()
    for copy in small:
        copy.wait()
    picks = sum(pick[i] for i in range(terms))
    inj_h, inj_t = newton(state[0], state[1], picks[:blocks], picks[blocks:2 * blocks], picks[2 * blocks:],
                          state[2], state[3])
    inj[0] = inj_h
    inj[1] = inj_t
    outs = [pltpu.make_async_copy(inj, inj_ref, in_sem.at[0])]
    outs[0].start()
    order = list(range(chips // 2, chips)) + list(range(chips // 2))
    pending = [None, None]
    for i, d in enumerate(order):
        slot = i % 2
        blk = (me >> 1) ^ d
        scale_h = jnp.broadcast_to(inj[0, pl.ds(blk, 1), :], (LANES, LANES)).T
        scale_t = jnp.broadcast_to(inj[1, pl.ds(blk, 1), :], (LANES, LANES)).T
        whole[d].wait()
        for copy in pending[slot] or ():
            copy.wait()
        for t in range(width):
            at = slice(t * LANES, (t + 1) * LANES)
            piece = pl.ds(t, LANES, stride=width)
            value = scale_h * rows[d, 0, piece, :] + scale_t * rows[d, 1, piece, :]
            dev[slot, :, at] = value
            unit[slot, at, :] = ((state[7, t:t + 1, :] + value) * (1.0 / math.pi)).T
        goal = dev_ref.at[pl.ds(pl.multiple_of(blk * LANES, LANES), LANES)]
        pending[slot] = stage([(dev.at[slot], goal), (unit.at[slot], units[d])], out_sem.at[slot])
    for copy in pending[0] + pending[1] + outs:
        copy.wait()


def prep_kernel(unit, chips, me_ref, from_ref, to_ref, slot_ref, sus_ref, rate_ref,
                f_ref, t_ref, ratio_ref, k_ref, cnt_ref):
    half = ratio_ref.shape[0]
    groups = half // GROUP
    me = me_ref[0]
    start = (me & 1) * half
    flip = me * unit
    bits = unit.bit_length() - 1
    slot = columns([slot_ref[...].astype(jnp.float32)])

    square = (LANES, LANES)
    before = lax.broadcasted_iota(jnp.int32, square, 0) < lax.broadcasted_iota(jnp.int32, square, 1)
    before = jnp.where(before, 1.0, 0.0).astype(jnp.bfloat16)
    lane = lax.broadcasted_iota(jnp.int32, (1, LANES), 1).astype(jnp.float32)
    slots = lax.broadcasted_iota(jnp.int32, (GROUP * LANES, LANES), 0).astype(jnp.float32)
    cnt_ref[...] = jnp.zeros_like(cnt_ref)

    def place(bus_ref, row):
        bus = jnp.concatenate([bus_ref[pl.ds(row + i, 1), :] for i in range(GROUP)], 1)
        rel = lookup(slot, bus)[0].astype(jnp.int32) ^ flip
        chip = rel >> (bits + 1)
        core = (rel >> bits) & 1
        return chip, (rel & (unit - 1)) + (core * chips + chip) * unit

    def group(g, carry):
        f_chip, f = place(from_ref, start + g * GROUP)
        t_chip, t = place(to_ref, start + g * GROUP)
        first = jnp.where(jnp.maximum(f_chip, t_chip) < chips - LATE, 1.0, 0.0)
        tile = lambda a, i: a[:, i * LANES:(i + 1) * LANES]
        flags = jnp.concatenate([tile(first, i) for i in range(GROUP)]
                                + [jnp.zeros((8 - GROUP, LANES), jnp.float32)], 0)
        ahead = jnp.dot(flags.astype(jnp.bfloat16), before, preferred_element_type=jnp.float32)
        sums = jnp.sum(flags, axis=1, keepdims=True)
        count = sum(sums[i:i + 1] for i in range(GROUP))
        offset = jnp.zeros((1, 1), jnp.float32)
        total = jnp.zeros((16, GROUP * LANES), jnp.float32)
        for i in range(GROUP):
            front = offset + ahead[i:i + 1]
            rest = count + (lane + float(i * LANES)) - front
            goal = jnp.where(tile(first, i) > 0.5, front, rest)
            offset = offset + sums[i:i + 1]
            hot = jnp.where(slots == goal, 1.0, 0.0).astype(jnp.bfloat16)
            row = pl.ds(start + g * GROUP + i, 1)
            rows = [tile(f, i) >> 7, tile(f, i) & 127, tile(t, i) >> 7, tile(t, i) & 127]
            rows = [r.astype(jnp.float32) for r in rows]
            rows += [p.astype(jnp.float32) for p in split(sus_ref[row, :] / rate_ref[row, :], 3)]
            rows += [jnp.full((1, LANES), float(i)), lane] + [jnp.zeros((1, LANES), jnp.float32)] * 7
            values = jnp.concatenate(rows, 0).astype(jnp.bfloat16)
            total += lax.dot_general(values, hot, (((1,), (1,)), ((), ())), preferred_element_type=jnp.float32)
        for i in range(GROUP):
            out = pl.ds(i * groups + g, 1)
            part = total[:, i * LANES:(i + 1) * LANES]
            f_ref[out, :] = (part[0:1] * 128.0 + part[1:2]).astype(jnp.int32)
            t_ref[out, :] = (part[2:3] * 128.0 + part[3:4]).astype(jnp.int32)
            ratio_ref[out, :] = part[4:5] + part[5:6] + part[6:7]
            origin = ((start + g * GROUP) * LANES).astype(jnp.float32)
            k_ref[out, :] = part[7:8] * 128.0 + part[8:9] + origin
        blocks = jnp.broadcast_to(count, (1, LANES)).astype(jnp.int32) >> 7
        cnt_ref[...] = jnp.where(lane == g.astype(jnp.float32), blocks, cnt_ref[...])
        return carry

    lax.fori_loop(0, half // GROUP, group, 0)


def join_kernel(_, *refs):
    pieces, (out_ref, sem) = refs[:-2], refs[-2:]
    unit = pieces[0].shape[0]
    for copy in stage([(p, out_ref.at[pl.ds(i * unit, unit)]) for i, p in enumerate(pieces)], sem):
        copy.wait()


def worst_kernel(late, me_ref, f_ref, t_ref, cnt_ref, ratio_ref, k_ref, state_ref, *rest):
    if late:
        best_ref, *rest = rest
    pieces, (out_ref, table, f_s, t_s, cnt_s, best, diff, sem) = rest[:2 * late + 2], rest[2 * late + 2:]
    half = f_ref.shape[0]
    groups = half // GROUP
    side = [pl.ds(0, half // 2), pl.ds(half // 2, half // 2)]
    main, spare = side[late], side[1 - late]
    pairs = [(cnt_ref, cnt_s), (f_ref.at[main], f_s.at[main]), (t_ref.at[main], t_s.at[main])]
    row = 0
    for own, other in zip(pieces[::2], pieces[1::2]):
        size = own.shape[0]
        pairs += [(own, table.at[pl.ds(row, size)]),
                  (other, table.at[pl.ds((table.shape[0] - SPARE) // 2 + row, size)])]
        row += size
    copies = stage(pairs, sem)
    ids = state_ref[6, pl.ds(me_ref[0] >> 1, 1), :]
    best[...] = best_ref[...] if late else jnp.zeros_like(best)
    for copy in copies:
        copy.wait()
    bound = cnt_s[0, 0]
    for g in range(1, groups):
        bound = jnp.minimum(bound, cnt_s[0, g]) if late else jnp.maximum(bound, cnt_s[0, g])

    @pl.when(bound < GROUP // 2 if late else bound > GROUP // 2)
    def _():
        for copy in stage([(f_ref.at[spare], f_s.at[spare]), (t_ref.at[spare], t_s.at[spare])], sem):
            copy.wait()

    def group(g, carry):
        def block(i, carry):
            b = i * groups + g
            for j in range(LANES):
                diff[pl.ds(j, 1), :] = table[pl.ds(f_s[b, j], 1), :] - table[pl.ds(t_s[b, j], 1), :]
            turn = diff[...]
            turn = turn - jnp.round(turn)
            square = turn * turn
            poly = SINE[4]
            for c in SINE[3::-1]:
                poly = poly * square + c
            scale = jnp.broadcast_to(ratio_ref[pl.ds(b, 1), :], (LANES, LANES)).T
            branch = jnp.broadcast_to(k_ref[pl.ds(b, 1), :], (LANES, LANES)).T
            load = jnp.where(branch == ids, 0.0, jnp.abs(turn * poly) * scale)
            best[...] = jnp.maximum(best[...], jnp.max(load.reshape(LANES // 8, 8, LANES), axis=0))
            return carry

        return lax.fori_loop(cnt_s[0, g] if late else 0, GROUP if late else cnt_s[0, g], block, carry)

    lax.fori_loop(0, groups, group, 0)
    out_ref[...] = jnp.max(best[...], axis=0, keepdims=True) if late else best[...]


def per_device(
    outages, branch_from, branch_to, bus_slot, susceptance, charging, rating, base_angles, zinv
):
    n_col = lax.axis_size("col")
    buses, cols = zinv.shape
    own = outages.shape[0]
    total = own * n_col
    blocks = total // LANES
    chips = n_col // 2
    assert own * 2 == LANES and cols // LANES <= blocks and chips & (chips - 1) == 0 and chips > 2
    me = lax.axis_index("col")
    where = me[None]
    tab = lambda a: a.reshape(-1, LANES)
    from2, to2, slot2, sus2, chg2, rate2, base2 = map(
        tab, (branch_from, branch_to, bus_slot, susceptance, charging, rating, base_angles)
    )
    i32 = lambda *s: jax.ShapeDtypeStruct(s, jnp.int32)
    f32 = lambda *s: jax.ShapeDtypeStruct(s, jnp.float32)

    flat = zinv.reshape(buses // 8, 8, cols // LANES, LANES).transpose(0, 2, 1, 3).reshape(-1, LANES)
    ids = lax.dynamic_update_slice(jnp.zeros((total,), jnp.int32), outages, (me * own,))
    ids = lax.psum(ids[None], "col")

    width = cols // LANES
    like = lambda a: pltpu.VMEM(a.shape, a.dtype)
    row_shape = (2, width * LANES, LANES)
    state, picks, rows = pl.pallas_call(
        functools.partial(ends_kernel, width),
        name="ends",
        out_shape=[f32(8, blocks, LANES), f32(3 * blocks, LANES), f32(blocks, *row_shape)],
        in_specs=[SMEM, VMEM] + [ANY] * 7,
        out_specs=[VMEM] * 2 + [ANY],
        scratch_shapes=[like(from2), like(to2), like(slot2), like(sus2), like(chg2), like(base2),
                        pltpu.VMEM((flat.shape[0] + SPARE, LANES), jnp.float32),
                        pltpu.VMEM((2 * blocks, LANES), jnp.int32), pltpu.SMEM((2 * blocks, LANES), jnp.int32),
                        pltpu.VMEM((2,) + row_shape, jnp.float32), pltpu.SemaphoreType.DMA((6,)),
                        pltpu.SemaphoreType.DMA((2,)), pltpu.SemaphoreType.DMA((CHUNKS,))],
        compiler_params=params(60),
    )(where, ids, from2, to2, slot2, sus2, chg2, base2, flat)

    swap = lambda a, m: lax.ppermute(a, "col", [(i, i ^ m) for i in range(n_col)])
    step = 1
    terms = [picks]
    while step < n_col:
        picks = sum(terms)
        terms = [picks] + [swap(picks, m * step) for m in range(1, min(4, n_col // step))]
        step *= 4

    nearby = state + jnp.minimum(me, 0).astype(jnp.float32)
    injections, deviation, *units = pl.pallas_call(
        functools.partial(spread_kernel, chips, len(terms)),
        name="spread",
        out_shape=[f32(2, blocks, LANES), f32(total, cols)] + [f32(cols, LANES)] * chips,
        in_specs=[SMEM] + [ANY] * (2 + len(terms)),
        out_specs=[ANY] * (2 + chips),
        scratch_shapes=[like(state), pltpu.VMEM((len(terms),) + picks.shape, jnp.float32),
                        pltpu.VMEM((2, blocks, LANES), jnp.float32), like(rows),
                        pltpu.VMEM((2, LANES, cols), jnp.float32), pltpu.VMEM((2, cols, LANES), jnp.float32),
                        pltpu.SemaphoreType.DMA((1 + len(terms),)), pltpu.SemaphoreType.DMA((chips,)),
                        pltpu.SemaphoreType.DMA((2, 2))],
        compiler_params=params(52),
    )(where, nearby, rows, *terms)

    half = branch_from.shape[0] // LANES // 2
    f_rel, t_rel, ratio, k_rel, counts = pl.pallas_call(
        functools.partial(prep_kernel, cols, chips),
        name="prep",
        out_shape=[i32(half, LANES), i32(half, LANES), f32(half, LANES), f32(half, LANES),
                   i32(1, LANES)],
        in_specs=[SMEM] + [VMEM] * 5,
        out_specs=[VMEM] * 5,
        compiler_params=params(16),
    )(where, from2, to2, slot2, sus2, rate2)

    got = [units[0]] + [swap(units[d], 2 * d) for d in range(1, chips)]

    def join(after, pieces):
        packed = pl.pallas_call(
            join_kernel,
            name="join",
            out_shape=f32(len(pieces) * cols, LANES),
            in_specs=[ANY] * (1 + len(pieces)),
            out_specs=VMEM,
            scratch_shapes=[pltpu.SemaphoreType.DMA((len(pieces),))],
            compiler_params=params(16),
        )(after, *pieces)
        return [packed, swap(packed, 1)]

    def worst_of(level, *operands):
        return pl.pallas_call(
            functools.partial(worst_kernel, level),
            name=f"worst{level}",
            out_shape=f32(1 if level else 8, LANES),
            in_specs=[SMEM] + [ANY] * 3 + [VMEM] * (3 + level) + [ANY] * (len(operands) - level),
            out_specs=VMEM,
            scratch_shapes=[pltpu.VMEM((buses + SPARE, LANES), jnp.float32), pltpu.SMEM(f_rel.shape, jnp.int32),
                            pltpu.SMEM(t_rel.shape, jnp.int32), pltpu.SMEM(counts.shape, jnp.int32),
                            pltpu.VMEM((8, LANES), jnp.float32), pltpu.VMEM((LANES, LANES), jnp.float32),
                            pltpu.SemaphoreType.DMA((3 + len(operands),))],
            compiler_params=params(16),
        )(where, f_rel, t_rel, counts, ratio, k_rel, state, *operands)

    early = join(counts, got[:-LATE])
    best = worst_of(0, *early)
    worst = worst_of(1, best, *early, *join(best, got[-LATE:]))
    mine = lambda a, b: lax.dynamic_slice(a, (jnp.int32(0),) * (a.ndim - len(b)) + b, a.shape[:1] + (1,) * (a.ndim - 2) + (own,))
    worst = jnp.maximum(mine(worst, ((me & 1) * own,)), mine(swap(worst, 1), ((me & 1) * own,))).reshape(own)
    inj = mine(injections, (me >> 1, (me & 1) * own)).reshape(2, own)
    return inj, deviation, worst


def solution(mesh):
    return jax.shard_map(
        per_device,
        mesh=mesh,
        in_specs=(P(("parts", "col")), P(), P(), P(), P(), P(), P(), P("parts"), P(None, "col")),
        out_specs=(P(None, ("parts", "col")), P("parts", "col"), P(("parts", "col"))),
        check_vma=False,
    )
```
